512 devices in a mesh: slab: 128 (over y, z, core), rep: 4 (over x).
Axes of the slice: x: 4, y: 4, z: 16, core: 2. Of those that a mesh axis runs over, the one named last changes fastest.
Arguments:
- camera_rows: float32 [655360, 128], P(('slab', 'rep')), may hold values from 0.1 to 4
- blend: float32 [655360], P(('slab', 'rep')), may hold values from 0.2 to 5
- route: int32 [655360], P(('slab', 'rep')), may hold values from 0 to 3, as said below
- line: int32 [655360], P(('slab', 'rep')), may hold values from 0 to 1023, as said below
- start: float32 [128, 1024, 512], P('slab', None, 'rep'), may hold values from 0.5 to 2
- psf_xy: float32 [31], replicated, may hold values from 0.05 to 1
- psf_z: float32 [63], replicated, may hold values from 0.05 to 1
Outputs:
- estimate: float32 [128, 1024, 512], P('slab', None, 'rep')
The draws below stay inside these ranges and needn't reach their ends.
Inputs may be any that keep to these rules, and one draw needn't show every extreme that they name: `route`: of the rows of one device, exactly 512 go to one owner, the same owner for all devices of one slab index, and exactly 256 to each other owner. A line is z * 1024 + x for local plane z of the owner. Every line of every owner is named by at least one row of its slab index.
All inputs are finite; a program needn't handle non-finite values.
Results may differ from the reference program's by a relative error of at most 0.0001.
Values sent between devices are 32-bit elements; how exact they have to be, the bound alone decides.
No kernel may reach another device: no remote copies, remote signals or barrier semaphores. Data moves between devices by JAX's collectives and lax.ppermute only.
A program may use at most 128 MiB of HBM per device.

```python
import math
import jax
import jax.numpy as jnp
from jax import lax

ZD = 1
X = 1024
YD = 128
TAPS_XY = 31
TAPS_Z = 63
ITERS = 2
Z = 128
Y = 512
LINES = 1024
SHARE = 256
ROWS_DEV = 1280
ROWS = 655360
N_SLAB = 128
N_REP = 4


def intersection_lists(key):
    devices = N_SLAB * N_REP
    heavy = jax.random.randint(jax.random.fold_in(key, 11), (N_SLAB,), 0, N_REP, dtype=jnp.int32)
    heavy_owner = jnp.repeat(heavy, N_REP)
    owner_base = jnp.repeat(jnp.arange(N_REP, dtype=jnp.int32), SHARE)
    owner_rows = jnp.broadcast_to(owner_base[None, :], (devices, N_REP * SHARE))
    line_keys = jax.random.split(jax.random.fold_in(key, 14), N_SLAB * N_REP)
    line_orders = jax.vmap(lambda single: jax.random.permutation(single, LINES))(line_keys).astype(jnp.int32)
    line_orders = line_orders.reshape(N_SLAB, N_REP, N_REP, SHARE)
    line_base = jnp.transpose(line_orders, (0, 2, 1, 3)).reshape(devices, N_REP * SHARE)
    extra_line = jax.random.randint(jax.random.fold_in(key, 12), (devices, SHARE), 0, LINES, dtype=jnp.int32)
    extra_owner = heavy_owner[:, None] * jnp.ones((devices, SHARE), jnp.int32)
    routes = jnp.concatenate([owner_rows, extra_owner], axis=1)
    lines = jnp.concatenate([line_base, extra_line], axis=1)
    order_keys = jax.random.split(jax.random.fold_in(key, 13), devices)
    orders = jax.vmap(lambda single: jax.random.permutation(single, ROWS_DEV))(order_keys).astype(jnp.int32)
    routes = jnp.take_along_axis(routes, orders, axis=1)
    lines = jnp.take_along_axis(lines, orders, axis=1)
    return (routes.reshape(-1).astype(jnp.int32), lines.reshape(-1).astype(jnp.int32))


def draw_route(key, part):
    return intersection_lists(key)[0]


def draw_line(key, part):
    return intersection_lists(key)[1]


def shard_levels(own_key, extent, cuts, smallest, top_value):
    def one(dim, shards_of):
        draws = jax.random.uniform(jax.random.fold_in(jax.random.fold_in(own_key, 6), dim), (shards_of,), jnp.float32, smallest / len(cuts), top_value / len(cuts))
        return jnp.repeat(jnp.exp(draws), extent[dim] // shards_of).reshape((-1,) + (1,) * (len(extent) - dim - 1))

    gain = one(*cuts[0])
    for cut in cuts[1:]:
        gain = gain * one(*cut)
    return gain


def setup_inputs(seed: int = 0) -> dict:
    streams_of = jax.random.split(jax.random.key(seed), 8)
    camera_rows = jnp.clip(jnp.exp(math.log(4.0) - 3.6888794 * jax.random.uniform(streams_of[0], (ROWS, YD), jnp.float32) ** shard_levels(streams_of[0], (ROWS, YD), ((0, 512),), -0.2, 0.2)), 0.1, 4.0)
    blend = jnp.clip(jnp.exp(math.log(5.0) - 3.218876 * jax.random.uniform(streams_of[1], (ROWS,), jnp.float32) ** shard_levels(streams_of[1], (ROWS,), ((0, 512),), -0.2, 0.2)), 0.2, 5.0)
    route = draw_route(jax.random.fold_in(streams_of[7], 71), 0)
    line = draw_line(jax.random.fold_in(streams_of[7], 71), 0)
    start = jnp.clip(jnp.exp(math.log(2.0) - 1.3862944 * jax.random.uniform(streams_of[4], (Z, X, Y), jnp.float32) ** shard_levels(streams_of[4], (Z, X, Y), ((0, 128), (2, 4)), -0.2, 0.2)), 0.5, 2.0)
    psf_xy = jnp.clip(jnp.exp(jax.random.uniform(streams_of[5], (TAPS_XY,), jnp.float32, math.log(0.05), math.log(1.0))), 0.05, 1.0)
    psf_z = jnp.clip(jnp.exp(jax.random.uniform(streams_of[6], (TAPS_Z,), jnp.float32, math.log(0.05), math.log(1.0))), 0.05, 1.0)
    return {"camera_rows": camera_rows, "blend": blend, "route": route, "line": line, "start": start, "psf_xy": psf_xy, "psf_z": psf_z}


def correlate(volume, psf_taps, axis):
    width = psf_taps.shape[0]
    half_width = width // 2
    moved = jnp.moveaxis(volume, axis, -1)
    shape = moved.shape
    flattened = moved.reshape(-1, 1, shape[-1])
    result = lax.conv_general_dilated(flattened, psf_taps.reshape(1, 1, width), (1,), [(half_width, half_width)], dimension_numbers=("NCH", "OIH", "NCH"), precision=lax.Precision.HIGHEST)
    return jnp.moveaxis(result.reshape(shape), -1, axis)


def reference(camera_rows, blend, route, line, start, psf_xy, psf_z):
    rows_all = camera_rows.shape[0]
    device_index = jnp.arange(rows_all, dtype=jnp.int32) // ROWS_DEV
    slab_index = device_index // N_REP
    plane_index = slab_index * ZD + line // X
    column_index = line % X
    cell_index = ((plane_index * X + column_index) * N_REP + route).astype(jnp.int32)
    weighted = camera_rows * blend[:, None]
    weighted_sum = jnp.zeros((Z * X * N_REP, YD), jnp.float32).at[cell_index].add(weighted)
    weight_sum = jnp.zeros((Z * X * N_REP,), jnp.float32).at[cell_index].add(blend)
    observed = (weighted_sum / weight_sum[:, None]).reshape(Z, X, N_REP * YD)
    h_xy = psf_xy / jnp.sum(psf_xy)
    h_z = psf_z / jnp.sum(psf_z)
    estimate = start
    for sweep in range(ITERS):
        blurred = correlate(correlate(correlate(estimate, h_xy, 1), h_xy, 2), h_z, 0)
        ratio = observed / blurred
        backed = correlate(correlate(correlate(ratio, h_z[::-1], 0), h_xy[::-1], 1), h_xy[::-1], 2)
        estimate = estimate * backed
    return estimate
```

```python
import functools

import jax
import jax.numpy as jnp
from jax import lax
from jax.experimental import pallas as pl
from jax.experimental.pallas import tpu as pltpu
from jax.sharding import PartitionSpec as P

F32 = jnp.float32
BF16 = jnp.bfloat16
LANES = 128
SIDE = 32
TAPS = 31
RIM = TAPS // 2
OWNERS = 4
CAPACITY = 512
META = 8
LINES = 1024
Z = 128
VMEM_LIMIT = 40 * 1024 * 1024


def call(kernel, out_shapes, scratch, *args, smem=0):
    specs = [
        pl.BlockSpec(memory_space=pltpu.SMEM if i < smem else pltpu.VMEM)
        for i in range(len(args))
    ]
    outs = tuple(jax.ShapeDtypeStruct(s, F32) for s in out_shapes)
    return pl.pallas_call(
        kernel,
        out_shape=outs,
        in_specs=specs,
        out_specs=tuple(pl.BlockSpec(memory_space=pltpu.VMEM) for _ in outs),
        scratch_shapes=[pltpu.VMEM(s, d) for s, d in scratch],
        compiler_params=pltpu.CompilerParams(vmem_limit_bytes=VMEM_LIMIT),
        name=kernel.func.__name__ if isinstance(kernel, functools.partial) else kernel.__name__,
    )(*args)


def halves(value):
    high = value.astype(BF16)
    return high, (value - high.astype(F32)).astype(BF16)


def thirds(value):
    high, rest = halves(value)
    low = (value - high.astype(F32) - rest.astype(F32)).astype(BF16)
    return high, rest, low


def lane_blocks(groups):
    block = lax.broadcasted_iota(jnp.int32, groups[0].shape, 2) // SIDE
    outs = []
    for sub in range(4):
        out = groups[sub]
        for j in range(4):
            if j != sub:
                moved = pltpu.roll(groups[j], (SIDE * (j - sub)) % LANES, axis=2)
                out = jnp.where(block == j, moved, out)
        outs.append(out)
    return outs


def store_tiles(plane, out_ref):
    cube = plane.reshape(32, SIDE, LANES)
    for sub, out in enumerate(lane_blocks([cube[:, 8 * j : 8 * j + 8, :] for j in range(4)])):
        out_ref[32 * sub : 32 * sub + 32] = out


def tiles_of_start(start_ref, taps_ref, out_ref, band_ref):
    store_tiles(start_ref[...], out_ref)
    rows = jnp.broadcast_to(taps_ref[...], (Z, LANES))
    rolled = pltpu.roll(rows, LANES - 31, axis=1, stride=1, stride_axis=0)
    j = lax.broadcasted_iota(jnp.int32, (Z, LANES), 0)
    z = lax.broadcasted_iota(jnp.int32, (Z, LANES), 1)
    band_ref[...] = jnp.where(jnp.abs(j - z) <= 31, rolled, 0.0)


def pack_rows(rows_ref, blend_ref, route_ref, line_ref, out_ref, split_ref, hot_ref):
    chunks = rows_ref.shape[0] // LANES
    blend = blend_ref[...]
    route = route_ref[...]
    line = line_ref[...]
    i = lax.broadcasted_iota(jnp.int32, (LANES, LANES), 0)
    j = lax.broadcasted_iota(jnp.int32, (LANES, LANES), 1)
    upto = (i <= j).astype(BF16)
    ones = jnp.ones((LANES, LANES), BF16)
    ci = lax.broadcasted_iota(jnp.int32, (16, 16), 0)
    cj = lax.broadcasted_iota(jnp.int32, (16, 16), 1)
    before = (cj < ci).astype(BF16)
    key = route * CAPACITY
    for owner in range(OWNERS):
        mine = (route == owner).astype(F32)
        mine16 = jnp.concatenate([mine, jnp.zeros((16 - chunks, LANES), F32)], axis=0).astype(BF16)
        upto_here = jnp.dot(mine16, upto, preferred_element_type=F32)
        totals = jnp.dot(mine16, ones, preferred_element_type=F32).astype(BF16)
        offset = jnp.dot(before, totals, preferred_element_type=F32)
        rank = (upto_here + offset)[:chunks] - 1.0
        key = key + jnp.where(route == owner, rank, 0.0).astype(jnp.int32)
    square = jnp.concatenate([blend, jnp.zeros((LANES - chunks, LANES), F32)], axis=0)
    columns = square.T
    for c in range(chunks):
        weighted = rows_ref[c * LANES : (c + 1) * LANES, :] * columns[:, c : c + 1]
        high, low = halves(weighted)
        split_ref[c * LANES : (c + 1) * LANES, :LANES] = high
        split_ref[c * LANES : (c + 1) * LANES, LANES:] = low
    first, second, third = thirds(blend)
    upper = line // 32
    parts = [first, second, third, upper.astype(BF16), (line - upper * 32).astype(BF16)]
    notes = jnp.concatenate(
        [
            jnp.concatenate(
                [p.astype(F32)[c : c + 1] for p in parts] + [jnp.zeros((3, LANES), F32)], axis=0
            )
            for c in range(chunks)
        ],
        axis=1,
    ).astype(BF16)
    for owner in range(OWNERS):
        slot = lax.broadcasted_iota(jnp.int32, (CAPACITY, LANES), 0) + owner * CAPACITY
        for c in range(chunks):
            hot = jnp.where(slot == key[c : c + 1, :], 1.0, 0.0)
            hot_ref[:, c * LANES : (c + 1) * LANES] = hot.astype(BF16)
        hot = hot_ref[...]
        both = jnp.dot(hot, split_ref[...], preferred_element_type=F32)
        out_ref[owner, :CAPACITY, :] = both[:, :LANES] + both[:, LANES:]
        meta = lax.dot_general(
            notes, hot, (((1,), (1,)), ((), ())), preferred_element_type=F32
        )
        weight = meta[0:1] + meta[1:2] + meta[2:3]
        where = meta[3:4] * 32.0 + meta[4:5]
        out_ref[owner, CAPACITY:, :] = jnp.concatenate(
            [weight[:, q * LANES : (q + 1) * LANES] for q in range(4)]
            + [where[:, q * LANES : (q + 1) * LANES] for q in range(4)],
            axis=0,
        )


def observe(got_ref, out_ref, hot_ref):
    total = jnp.zeros((LINES, 2 * LANES), F32)
    weights = jnp.zeros((LINES, 8), F32)
    at = lax.broadcasted_iota(jnp.int32, (LINES, LANES), 0)
    for source in range(OWNERS):
        meta = got_ref[source, CAPACITY:, :]
        where = meta[4:8].astype(jnp.int32)
        for q in range(4):
            hot = jnp.where(at == where[q : q + 1, :], 1.0, 0.0)
            hot_ref[:, q * LANES : (q + 1) * LANES] = hot.astype(BF16)
        hot = hot_ref[...]
        high, low = halves(got_ref[source, :CAPACITY, :])
        total += jnp.dot(hot, jnp.concatenate([high, low], axis=1), preferred_element_type=F32)
        weight = jnp.concatenate([meta[q : q + 1] for q in range(4)], axis=1)
        parts = [p.astype(F32) for p in thirds(weight)]
        stacked = jnp.concatenate(parts + [jnp.zeros((5, CAPACITY), F32)], axis=0).astype(BF16)
        weights += lax.dot_general(
            hot, stacked, (((1,), (1,)), ((), ())), preferred_element_type=F32
        )
    weight_sum = weights[:, 0:1] + weights[:, 1:2] + weights[:, 2:3]
    store_tiles((total[:, :LANES] + total[:, LANES:]) / weight_sum, out_ref)


def columns_from(got_ref, out_ref):
    for i in range(8):
        turned = got_ref[pl.ds(i, Z, stride=8), :].T
        for j in range(4):
            out_ref[8 * j + i] = turned[SIDE * j : SIDE * j + SIDE, :]


def arrive(got_ref, out_ref, low_ref, high_ref):
    columns_from(got_ref, out_ref)
    low_ref[...] = out_ref[:RIM]
    high_ref[...] = out_ref[SIDE - RIM :]


def convolve(taps_ref, flip, low_ref, mid_ref, high_ref, wide_ref, flat_ref):
    wide_ref[:RIM] = low_ref[...]
    wide_ref[RIM : RIM + SIDE] = mid_ref[...]
    wide_ref[RIM + SIDE :] = high_ref[...]
    taps = [taps_ref[TAPS - 1 - k if flip else k] for k in range(TAPS)]

    def block(index, carry):
        lead = (index // 4) * 8
        row = pl.multiple_of((index % 4) * 8, 8)
        total = taps[0] * wide_ref[pl.ds(lead, 8), pl.ds(row, 8), :]
        for k in range(1, TAPS):
            total = total + taps[k] * wide_ref[pl.ds(lead + k, 8), pl.ds(row, 8), :]
        for i in range(8):
            flat_ref[pl.ds(pl.multiple_of((lead + i) * SIDE + row, 8), 8), :] = total[i]
        return carry

    lax.fori_loop(0, 16, block, 0)


def along_x(flip, taps_ref, low_ref, mid_ref, high_ref, out_ref, first_ref, last_ref, wide_ref, flat_ref):
    convolve(taps_ref, flip, low_ref, mid_ref, high_ref, wide_ref, flat_ref)
    for y in range(SIDE):
        out_ref[y] = flat_ref[pl.ds(y, SIDE, stride=SIDE), :]
    first_ref[...] = out_ref[:RIM]
    last_ref[...] = out_ref[SIDE - RIM :]


def along_y(taps_ref, flip, low_ref, mid_ref, high_ref, wide_ref, flat_ref, out_ref):
    convolve(taps_ref, flip, low_ref, mid_ref, high_ref, wide_ref, flat_ref)
    for x in range(SIDE):
        out_ref[SIDE * x : SIDE * x + SIDE, :] = flat_ref[pl.ds(x, SIDE, stride=SIDE), :]


def axial(value, band, back):
    return lax.dot_general(
        value,
        band,
        (((1,), (1 if back else 0,)), ((), ())),
        precision=lax.Precision.HIGHEST,
        preferred_element_type=F32,
    )


def blur(taps_ref, low_ref, mid_ref, high_ref, band_ref, out_ref, wide_ref, flat_ref, cols_ref):
    along_y(taps_ref, False, low_ref, mid_ref, high_ref, wide_ref, flat_ref, cols_ref)
    out_ref[...] = axial(cols_ref[...], band_ref[...], False)


def back_axial(ratio, band_ref, out_ref, first_ref, last_ref):
    back = axial(ratio, band_ref[...], True)
    out_ref[...] = back.reshape(SIDE, SIDE, Z)
    first_ref[...] = back[: RIM * SIDE].reshape(RIM, SIDE, Z)
    last_ref[...] = back[(SIDE - RIM) * SIDE :].reshape(RIM, SIDE, Z)


def first_ratio(got_ref, blurred_ref, band_ref, seen_ref, out_ref, first_ref, last_ref):
    columns_from(got_ref, seen_ref)
    ratio = seen_ref[...].reshape(SIDE * SIDE, Z) / blurred_ref[...]
    back_axial(ratio, band_ref, out_ref, first_ref, last_ref)


def blur_ratio(
    taps_ref, low_ref, mid_ref, high_ref, band_ref, seen_ref, out_ref, first_ref, last_ref, wide_ref, flat_ref, cols_ref
):
    along_y(taps_ref, False, low_ref, mid_ref, high_ref, wide_ref, flat_ref, cols_ref)
    blurred = axial(cols_ref[...], band_ref[...], False)
    back_axial(seen_ref[...].reshape(SIDE * SIDE, Z) / blurred, band_ref, out_ref, first_ref, last_ref)


def update(
    taps_ref, low_ref, mid_ref, high_ref, estimate_ref, out_ref, first_ref, last_ref, wide_ref, flat_ref, cols_ref
):
    along_y(taps_ref, True, low_ref, mid_ref, high_ref, wide_ref, flat_ref, cols_ref)
    out_ref[...] = estimate_ref[...] * cols_ref[...].reshape(SIDE, SIDE, Z)
    first_ref[...] = out_ref[:RIM]
    last_ref[...] = out_ref[SIDE - RIM :]


def last_update(
    taps_ref, low_ref, mid_ref, high_ref, estimate_ref, out_ref, wide_ref, flat_ref, cols_ref
):
    along_y(taps_ref, True, low_ref, mid_ref, high_ref, wide_ref, flat_ref, cols_ref)
    for i in range(8):
        block = jnp.concatenate(
            [
                estimate_ref[8 * j + i] * cols_ref[SIDE * (8 * j + i) : SIDE * (8 * j + i) + SIDE, :]
                for j in range(4)
            ],
            axis=0,
        )
        out_ref[pl.ds(i, Z, stride=8), :] = block.T


def plane_of(got_ref, out_ref):
    outs = lane_blocks([got_ref[32 * sub : 32 * sub + 32] for sub in range(4)])
    for j, out in enumerate(outs):
        out_ref[:, 8 * j : 8 * j + 8, :] = out


TILE = (SIDE, SIDE, Z)
EDGE = (RIM, SIDE, Z)
PIECES = (Z, 8, LANES)
FLAT = (SIDE * SIDE, Z)
SCRATCH = [((SIDE + 2 * RIM, SIDE, Z), F32), (FLAT, F32), (FLAT, F32)]


def exchange(first, last, pairs, axes):
    low = lax.ppermute(last, axes, pairs)
    high = lax.ppermute(first, axes, [(b, a) for a, b in pairs])
    return low, high


def shards(camera_rows, blend, route, line, start, psf_xy, psf_z):
    slabs, reps = lax.axis_size("slab"), lax.axis_size("rep")
    x_tiles = LINES // SIDE
    y_tiles = slabs // x_tiles
    chunks = camera_rows.shape[0] // LANES
    x_pairs = [(t, t + 1) for t in range(slabs) if t % x_tiles != x_tiles - 1]
    y_pairs = []
    for t in range(slabs):
        for r in range(reps):
            y = r * y_tiles + t // x_tiles + 1
            if y < y_tiles * reps:
                up = (y % y_tiles) * x_tiles + t % x_tiles
                y_pairs.append((t * reps + r, up * reps + y // y_tiles))

    def rims_x(first, last):
        return exchange(first, last, x_pairs, "slab")

    def rims_y(first, last):
        return exchange(first, last, y_pairs, ("slab", "rep"))

    def turn(pieces):
        return lax.all_to_all(pieces, "slab", split_axis=0, concat_axis=0, tiled=True)

    taps = psf_xy / jnp.sum(psf_xy)
    taps_z = jnp.pad((psf_z / jnp.sum(psf_z))[::-1], (0, LANES - psf_z.shape[0]))[None, :]

    sent = call(
        pack_rows,
        [(OWNERS, CAPACITY + META, LANES)],
        [((chunks * LANES, 2 * LANES), BF16), ((CAPACITY, chunks * LANES), BF16)],
        camera_rows,
        blend.reshape(chunks, LANES),
        route.reshape(chunks, LANES),
        line.reshape(chunks, LANES),
    )[0]
    got = lax.all_to_all(sent, "rep", split_axis=0, concat_axis=0, tiled=True)
    pieces, band = call(
        tiles_of_start, [PIECES, (Z, LANES)], [], start.reshape(LINES, LANES), taps_z
    )
    arrived = turn(pieces)
    seen_pieces = call(observe, [PIECES], [((LINES, CAPACITY), BF16)], got)[0]
    seen_arrived = turn(seen_pieces)

    estimate, first, last = call(
        arrive, [TILE, EDGE, EDGE], [], arrived.reshape(Z * 8, LANES)
    )

    def lateral_x(flip, value, first, last):
        low, high = rims_x(first, last)
        value, first, last = call(
            functools.partial(along_x, flip), [TILE, EDGE, EDGE], SCRATCH[:2], taps, low, value, high, smem=1
        )
        low, high = rims_y(first, last)
        return low, value, high

    wide = lateral_x(False, estimate, first, last)
    blurred = call(blur, [FLAT], SCRATCH, taps, *wide, band, smem=1)[0]
    seen, back, first, last = call(
        first_ratio, [TILE, TILE, EDGE, EDGE], [], seen_arrived.reshape(Z * 8, LANES), blurred, band
    )
    wide = lateral_x(True, back, first, last)
    estimate, first, last = call(
        update, [TILE, EDGE, EDGE], SCRATCH, taps, *wide, estimate, smem=1
    )
    wide = lateral_x(False, estimate, first, last)
    back, first, last = call(
        blur_ratio, [TILE, EDGE, EDGE], SCRATCH, taps, *wide, band, seen, smem=1
    )
    wide = lateral_x(True, back, first, last)
    pieces = call(last_update, [(Z * 8, LANES)], SCRATCH, taps, *wide, estimate, smem=1)[0]
    done = turn(pieces.reshape(PIECES))
    plane = call(plane_of, [(LINES // SIDE, SIDE, LANES)], [], done)[0]
    return plane.reshape(1, LINES, LANES)


def solution(mesh):
    in_specs = (
        P(("slab", "rep"), None),
        P(("slab", "rep")),
        P(("slab", "rep")),
        P(("slab", "rep")),
        P("slab", None, "rep"),
        P(),
        P(),
    )
    out_specs = P("slab", None, "rep")
    return jax.shard_map(shards, mesh=mesh, in_specs=in_specs, out_specs=out_specs, check_vma=False)
```

```python
import functools

import jax
import jax.numpy as jnp
from jax import lax
from jax.experimental import pallas as pl
from jax.experimental.pallas import tpu as pltpu
from jax.sharding import PartitionSpec as P

F32 = jnp.float32
BF16 = jnp.bfloat16
LANES = 128
SIDE = 32
TAPS = 31
RIM = TAPS // 2
OWNERS = 4
CAPACITY = 512
META = 8
LINES = 1024
Z = 128
VMEM_LIMIT = 40 * 1024 * 1024


def call(kernel, out_shapes, scratch, *args, smem=0):
    specs = [
        pl.BlockSpec(memory_space=pltpu.SMEM if i < smem else pltpu.VMEM)
        for i in range(len(args))
    ]
    outs = tuple(jax.ShapeDtypeStruct(s, F32) for s in out_shapes)
    return pl.pallas_call(
        kernel,
        out_shape=outs,
        in_specs=specs,
        out_specs=tuple(pl.BlockSpec(memory_space=pltpu.VMEM) for _ in outs),
        scratch_shapes=[pltpu.VMEM(s, d) for s, d in scratch],
        compiler_params=pltpu.CompilerParams(vmem_limit_bytes=VMEM_LIMIT),
        name=kernel.func.__name__ if isinstance(kernel, functools.partial) else kernel.__name__,
    )(*args)


def halves(value):
    high = value.astype(BF16)
    return high, (value - high.astype(F32)).astype(BF16)


def thirds(value):
    high, rest = halves(value)
    low = (value - high.astype(F32) - rest.astype(F32)).astype(BF16)
    return high, rest, low


def lane_blocks(groups):
    block = lax.broadcasted_iota(jnp.int32, groups[0].shape, 2) // SIDE
    outs = []
    for sub in range(4):
        out = groups[sub]
        for j in range(4):
            if j != sub:
                moved = pltpu.roll(groups[j], (SIDE * (j - sub)) % LANES, axis=2)
                out = jnp.where(block == j, moved, out)
        outs.append(out)
    return outs


def store_tiles(plane, out_ref):
    cube = plane.reshape(32, SIDE, LANES)
    for sub, out in enumerate(lane_blocks([cube[:, 8 * j : 8 * j + 8, :] for j in range(4)])):
        out_ref[32 * sub : 32 * sub + 32] = out


def tiles_of_start(start_ref, taps_ref, out_ref, band_ref):
    store_tiles(start_ref[...], out_ref)
    rows = jnp.broadcast_to(taps_ref[...], (Z, LANES))
    rolled = pltpu.roll(rows, LANES - 31, axis=1, stride=1, stride_axis=0)
    j = lax.broadcasted_iota(jnp.int32, (Z, LANES), 0)
    z = lax.broadcasted_iota(jnp.int32, (Z, LANES), 1)
    band_ref[...] = jnp.where(jnp.abs(j - z) <= 31, rolled, 0.0)


def pack_rows(rep_ref, rows_ref, blend_ref, route_ref, line_ref, *refs):
    out_refs, (split_ref, hot_ref) = refs[:OWNERS], refs[OWNERS:]
    chunks = rows_ref.shape[0] // LANES
    blend = blend_ref[...]
    route = route_ref[...]
    line = line_ref[...]
    i = lax.broadcasted_iota(jnp.int32, (LANES, LANES), 0)
    j = lax.broadcasted_iota(jnp.int32, (LANES, LANES), 1)
    upto = (i <= j).astype(BF16)
    ones = jnp.ones((LANES, LANES), BF16)
    ci = lax.broadcasted_iota(jnp.int32, (16, 16), 0)
    cj = lax.broadcasted_iota(jnp.int32, (16, 16), 1)
    before = (cj < ci).astype(BF16)
    key = route * CAPACITY
    for owner in range(OWNERS):
        mine = (route == owner).astype(F32)
        mine16 = jnp.concatenate([mine, jnp.zeros((16 - chunks, LANES), F32)], axis=0).astype(BF16)
        upto_here = jnp.dot(mine16, upto, preferred_element_type=F32)
        totals = jnp.dot(mine16, ones, preferred_element_type=F32).astype(BF16)
        offset = jnp.dot(before, totals, preferred_element_type=F32)
        rank = (upto_here + offset)[:chunks] - 1.0
        key = key + jnp.where(route == owner, rank, 0.0).astype(jnp.int32)
    square = jnp.concatenate([blend, jnp.zeros((LANES - chunks, LANES), F32)], axis=0)
    columns = square.T
    for c in range(chunks):
        weighted = rows_ref[c * LANES : (c + 1) * LANES, :] * columns[:, c : c + 1]
        high, low = halves(weighted)
        split_ref[c * LANES : (c + 1) * LANES, :LANES] = high
        split_ref[c * LANES : (c + 1) * LANES, LANES:] = low
    first, second, third = thirds(blend)
    upper = line // 32
    parts = [first, second, third, upper.astype(BF16), (line - upper * 32).astype(BF16)]
    notes = jnp.concatenate(
        [
            jnp.concatenate(
                [p.astype(F32)[c : c + 1] for p in parts] + [jnp.zeros((3, LANES), F32)], axis=0
            )
            for c in range(chunks)
        ],
        axis=1,
    ).astype(BF16)
    for step, out_ref in enumerate(out_refs):
        owner = (rep_ref[0] + step) % OWNERS
        slot = lax.broadcasted_iota(jnp.int32, (CAPACITY, LANES), 0) + owner * CAPACITY
        for c in range(chunks):
            hot = jnp.where(slot == key[c : c + 1, :], 1.0, 0.0)
            hot_ref[:, c * LANES : (c + 1) * LANES] = hot.astype(BF16)
        hot = hot_ref[...]
        both = jnp.dot(hot, split_ref[...], preferred_element_type=F32)
        out_ref[:CAPACITY, :] = both[:, :LANES] + both[:, LANES:]
        meta = lax.dot_general(
            notes, hot, (((1,), (1,)), ((), ())), preferred_element_type=F32
        )
        weight = meta[0:1] + meta[1:2] + meta[2:3]
        where = meta[3:4] * 32.0 + meta[4:5]
        out_ref[CAPACITY:, :] = jnp.concatenate(
            [weight[:, q * LANES : (q + 1) * LANES] for q in range(4)]
            + [where[:, q * LANES : (q + 1) * LANES] for q in range(4)],
            axis=0,
        )


def observe(*refs):
    got_refs, (out_ref, hot_ref) = refs[:OWNERS], refs[OWNERS:]
    total = jnp.zeros((LINES, 2 * LANES), F32)
    weights = jnp.zeros((LINES, 8), F32)
    at = lax.broadcasted_iota(jnp.int32, (LINES, LANES), 0)
    for got_ref in got_refs:
        meta = got_ref[CAPACITY:, :]
        where = meta[4:8].astype(jnp.int32)
        for q in range(4):
            hot = jnp.where(at == where[q : q + 1, :], 1.0, 0.0)
            hot_ref[:, q * LANES : (q + 1) * LANES] = hot.astype(BF16)
        hot = hot_ref[...]
        high, low = halves(got_ref[:CAPACITY, :])
        total += jnp.dot(hot, jnp.concatenate([high, low], axis=1), preferred_element_type=F32)
        weight = jnp.concatenate([meta[q : q + 1] for q in range(4)], axis=1)
        parts = [p.astype(F32) for p in thirds(weight)]
        stacked = jnp.concatenate(parts + [jnp.zeros((5, CAPACITY), F32)], axis=0).astype(BF16)
        weights += lax.dot_general(
            hot, stacked, (((1,), (1,)), ((), ())), preferred_element_type=F32
        )
    weight_sum = weights[:, 0:1] + weights[:, 1:2] + weights[:, 2:3]
    store_tiles((total[:, :LANES] + total[:, LANES:]) / weight_sum, out_ref)


def columns_from(got_ref, out_ref):
    for i in range(8):
        turned = got_ref[pl.ds(i, Z, stride=8), :].T
        for j in range(4):
            out_ref[8 * j + i] = turned[SIDE * j : SIDE * j + SIDE, :]


def arrive(got_ref, out_ref, low_ref, high_ref):
    columns_from(got_ref, out_ref)
    low_ref[...] = out_ref[:RIM]
    high_ref[...] = out_ref[SIDE - RIM :]


def convolve(taps_ref, flip, low_ref, mid_ref, high_ref, wide_ref, flat_ref):
    wide_ref[:RIM] = low_ref[...]
    wide_ref[RIM : RIM + SIDE] = mid_ref[...]
    wide_ref[RIM + SIDE :] = high_ref[...]
    taps = [taps_ref[TAPS - 1 - k if flip else k] for k in range(TAPS)]

    def block(index, carry):
        lead = (index // 4) * 8
        row = pl.multiple_of((index % 4) * 8, 8)
        total = taps[0] * wide_ref[pl.ds(lead, 8), pl.ds(row, 8), :]
        for k in range(1, TAPS):
            total = total + taps[k] * wide_ref[pl.ds(lead + k, 8), pl.ds(row, 8), :]
        for i in range(8):
            flat_ref[pl.ds(pl.multiple_of((lead + i) * SIDE + row, 8), 8), :] = total[i]
        return carry

    lax.fori_loop(0, 16, block, 0)


def along_x(flip, taps_ref, low_ref, mid_ref, high_ref, out_ref, first_ref, last_ref, wide_ref, flat_ref):
    convolve(taps_ref, flip, low_ref, mid_ref, high_ref, wide_ref, flat_ref)
    for y in range(SIDE):
        out_ref[y] = flat_ref[pl.ds(y, SIDE, stride=SIDE), :]
    first_ref[...] = out_ref[:RIM]
    last_ref[...] = out_ref[SIDE - RIM :]


def along_y(taps_ref, flip, low_ref, mid_ref, high_ref, wide_ref, flat_ref, out_ref):
    convolve(taps_ref, flip, low_ref, mid_ref, high_ref, wide_ref, flat_ref)
    for x in range(SIDE):
        out_ref[SIDE * x : SIDE * x + SIDE, :] = flat_ref[pl.ds(x, SIDE, stride=SIDE), :]


def axial(value, band, back):
    return lax.dot_general(
        value,
        band,
        (((1,), (1 if back else 0,)), ((), ())),
        precision=lax.Precision.HIGHEST,
        preferred_element_type=F32,
    )


def blur(taps_ref, low_ref, mid_ref, high_ref, band_ref, out_ref, wide_ref, flat_ref, cols_ref):
    along_y(taps_ref, False, low_ref, mid_ref, high_ref, wide_ref, flat_ref, cols_ref)
    out_ref[...] = axial(cols_ref[...], band_ref[...], False)


def back_axial(ratio, band_ref, out_ref, first_ref, last_ref):
    back = axial(ratio, band_ref[...], True)
    out_ref[...] = back.reshape(SIDE, SIDE, Z)
    first_ref[...] = back[: RIM * SIDE].reshape(RIM, SIDE, Z)
    last_ref[...] = back[(SIDE - RIM) * SIDE :].reshape(RIM, SIDE, Z)


def first_ratio(got_ref, blurred_ref, band_ref, seen_ref, out_ref, first_ref, last_ref):
    columns_from(got_ref, seen_ref)
    ratio = seen_ref[...].reshape(SIDE * SIDE, Z) / blurred_ref[...]
    back_axial(ratio, band_ref, out_ref, first_ref, last_ref)


def blur_ratio(
    taps_ref, low_ref, mid_ref, high_ref, band_ref, seen_ref, out_ref, first_ref, last_ref, wide_ref, flat_ref, cols_ref
):
    along_y(taps_ref, False, low_ref, mid_ref, high_ref, wide_ref, flat_ref, cols_ref)
    blurred = axial(cols_ref[...], band_ref[...], False)
    back_axial(seen_ref[...].reshape(SIDE * SIDE, Z) / blurred, band_ref, out_ref, first_ref, last_ref)


def update(
    taps_ref, low_ref, mid_ref, high_ref, estimate_ref, out_ref, first_ref, last_ref, wide_ref, flat_ref, cols_ref
):
    along_y(taps_ref, True, low_ref, mid_ref, high_ref, wide_ref, flat_ref, cols_ref)
    out_ref[...] = estimate_ref[...] * cols_ref[...].reshape(SIDE, SIDE, Z)
    first_ref[...] = out_ref[:RIM]
    last_ref[...] = out_ref[SIDE - RIM :]


def last_update(
    taps_ref, low_ref, mid_ref, high_ref, estimate_ref, out_ref, wide_ref, flat_ref, cols_ref
):
    along_y(taps_ref, True, low_ref, mid_ref, high_ref, wide_ref, flat_ref, cols_ref)
    for i in range(8):
        block = jnp.concatenate(
            [
                estimate_ref[8 * j + i] * cols_ref[SIDE * (8 * j + i) : SIDE * (8 * j + i) + SIDE, :]
                for j in range(4)
            ],
            axis=0,
        )
        out_ref[pl.ds(i, Z, stride=8), :] = block.T


def plane_of(got_ref, out_ref):
    outs = lane_blocks([got_ref[32 * sub : 32 * sub + 32] for sub in range(4)])
    for j, out in enumerate(outs):
        out_ref[:, 8 * j : 8 * j + 8, :] = out


TILE = (SIDE, SIDE, Z)
EDGE = (RIM, SIDE, Z)
PIECES = (Z, 8, LANES)
FLAT = (SIDE * SIDE, Z)
SCRATCH = [((SIDE + 2 * RIM, SIDE, Z), F32), (FLAT, F32), (FLAT, F32)]


def exchange(first, last, pairs, axes):
    low = lax.ppermute(last, axes, pairs)
    high = lax.ppermute(first, axes, [(b, a) for a, b in pairs])
    return low, high


def shards(camera_rows, blend, route, line, start, psf_xy, psf_z):
    slabs, reps = lax.axis_size("slab"), lax.axis_size("rep")
    x_tiles = LINES // SIDE
    y_tiles = slabs // x_tiles
    chunks = camera_rows.shape[0] // LANES
    x_pairs = [(t, t + 1) for t in range(slabs) if t % x_tiles != x_tiles - 1]
    y_pairs = []
    for t in range(slabs):
        for r in range(reps):
            y = r * y_tiles + t // x_tiles + 1
            if y < y_tiles * reps:
                up = (y % y_tiles) * x_tiles + t % x_tiles
                y_pairs.append((t * reps + r, up * reps + y // y_tiles))

    def rims_x(first, last):
        return exchange(first, last, x_pairs, "slab")

    def rims_y(first, last):
        return exchange(first, last, y_pairs, ("slab", "rep"))

    def turn(pieces):
        return lax.all_to_all(pieces, "slab", split_axis=0, concat_axis=0, tiled=True)

    taps = psf_xy / jnp.sum(psf_xy)
    taps_z = jnp.pad((psf_z / jnp.sum(psf_z))[::-1], (0, LANES - psf_z.shape[0]))[None, :]

    pieces, band = call(
        tiles_of_start, [PIECES, (Z, LANES)], [], start.reshape(LINES, LANES), taps_z
    )
    arrived = turn(pieces)
    sent = call(
        pack_rows,
        [(CAPACITY + META, LANES)] * OWNERS,
        [((chunks * LANES, 2 * LANES), BF16), ((CAPACITY, chunks * LANES), BF16)],
        lax.axis_index("rep").reshape(1),
        camera_rows,
        blend.reshape(chunks, LANES),
        route.reshape(chunks, LANES),
        line.reshape(chunks, LANES),
        smem=1,
    )
    got = [
        block if step == 0 else lax.ppermute(block, "rep", [(r, (r + step) % reps) for r in range(reps)])
        for step, block in enumerate(sent)
    ]
    seen_pieces = call(observe, [PIECES], [((LINES, CAPACITY), BF16)], *got)[0]
    seen_arrived = turn(seen_pieces)

    estimate, first, last = call(
        arrive, [TILE, EDGE, EDGE], [], arrived.reshape(Z * 8, LANES)
    )

    def lateral_x(flip, value, first, last):
        low, high = rims_x(first, last)
        value, first, last = call(
            functools.partial(along_x, flip), [TILE, EDGE, EDGE], SCRATCH[:2], taps, low, value, high, smem=1
        )
        low, high = rims_y(first, last)
        return low, value, high

    wide = lateral_x(False, estimate, first, last)
    blurred = call(blur, [FLAT], SCRATCH, taps, *wide, band, smem=1)[0]
    seen, back, first, last = call(
        first_ratio, [TILE, TILE, EDGE, EDGE], [], seen_arrived.reshape(Z * 8, LANES), blurred, band
    )
    wide = lateral_x(True, back, first, last)
    estimate, first, last = call(
        update, [TILE, EDGE, EDGE], SCRATCH, taps, *wide, estimate, smem=1
    )
    wide = lateral_x(False, estimate, first, last)
    back, first, last = call(
        blur_ratio, [TILE, EDGE, EDGE], SCRATCH, taps, *wide, band, seen, smem=1
    )
    wide = lateral_x(True, back, first, last)
    pieces = call(last_update, [(Z * 8, LANES)], SCRATCH, taps, *wide, estimate, smem=1)[0]
    done = turn(pieces.reshape(PIECES))
    plane = call(plane_of, [(LINES // SIDE, SIDE, LANES)], [], done)[0]
    return plane.reshape(1, LINES, LANES)


def solution(mesh):
    in_specs = (
        P(("slab", "rep"), None),
        P(("slab", "rep")),
        P(("slab", "rep")),
        P(("slab", "rep")),
        P("slab", None, "rep"),
        P(),
        P(),
    )
    out_specs = P("slab", None, "rep")
    return jax.shard_map(shards, mesh=mesh, in_specs=in_specs, out_specs=out_specs, check_vma=False)
```

```python
import functools

import jax
import jax.numpy as jnp
from jax import lax
from jax.experimental import pallas as pl
from jax.experimental.pallas import tpu as pltpu
from jax.sharding import PartitionSpec as P

F32 = jnp.float32
BF16 = jnp.bfloat16
LANES = 128
SIDE = 32
TAPS = 31
RIM = TAPS // 2
OWNERS = 4
CAPACITY = 512
META = 8
LINES = 1024
Z = 128
VMEM_LIMIT = 40 * 1024 * 1024


def call(kernel, out_shapes, scratch, *args, smem=0):
    specs = [
        pl.BlockSpec(memory_space=pltpu.SMEM if i < smem else pltpu.VMEM)
        for i in range(len(args))
    ]
    outs = tuple(jax.ShapeDtypeStruct(s, F32) for s in out_shapes)
    return pl.pallas_call(
        kernel,
        out_shape=outs,
        in_specs=specs,
        out_specs=tuple(pl.BlockSpec(memory_space=pltpu.VMEM) for _ in outs),
        scratch_shapes=[pltpu.VMEM(s, d) for s, d in scratch],
        compiler_params=pltpu.CompilerParams(vmem_limit_bytes=VMEM_LIMIT),
        name=kernel.func.__name__ if isinstance(kernel, functools.partial) else kernel.__name__,
    )(*args)


def halves(value):
    high = value.astype(BF16)
    return high, (value - high.astype(F32)).astype(BF16)


def thirds(value):
    high, rest = halves(value)
    low = (value - high.astype(F32) - rest.astype(F32)).astype(BF16)
    return high, rest, low


def lane_blocks(groups):
    block = lax.broadcasted_iota(jnp.int32, groups[0].shape, 2) // SIDE
    outs = []
    for sub in range(4):
        out = groups[sub]
        for j in range(4):
            if j != sub:
                moved = pltpu.roll(groups[j], (SIDE * (j - sub)) % LANES, axis=2)
                out = jnp.where(block == j, moved, out)
        outs.append(out)
    return outs


def store_tiles(plane, out_ref):
    cube = plane.reshape(32, SIDE, LANES)
    for sub, out in enumerate(lane_blocks([cube[:, 8 * j : 8 * j + 8, :] for j in range(4)])):
        out_ref[32 * sub : 32 * sub + 32] = out


def tiles_of_start(start_ref, out_ref):
    store_tiles(start_ref[...], out_ref)


def axial_band(psf_ref, out_ref, row_ref):
    row_ref[...] = jnp.zeros((8, LANES), F32)
    row_ref[0:1, : psf_ref.shape[1]] = psf_ref[...]
    psf = row_ref[0:1, :]
    rows = jnp.broadcast_to(psf / jnp.sum(psf, axis=1, keepdims=True), (Z, LANES))
    rolled = pltpu.roll(rows, LANES - 31, axis=1, stride=1, stride_axis=0)
    a = lax.broadcasted_iota(jnp.int32, (Z, LANES), 0)
    b = lax.broadcasted_iota(jnp.int32, (Z, LANES), 1)
    out_ref[...] = jnp.where(jnp.abs(a - b) <= 31, rolled, 0.0)


def pack_rows(rep_ref, rows_ref, blend_ref, route_ref, line_ref, *refs):
    out_refs, (split_ref, hot_ref) = refs[:OWNERS], refs[OWNERS:]
    chunks = rows_ref.shape[0] // LANES
    blend = blend_ref[...]
    route = route_ref[...]
    line = line_ref[...]
    i = lax.broadcasted_iota(jnp.int32, (LANES, LANES), 0)
    j = lax.broadcasted_iota(jnp.int32, (LANES, LANES), 1)
    upto = (i <= j).astype(BF16)
    ones = jnp.ones((LANES, LANES), BF16)
    ci = lax.broadcasted_iota(jnp.int32, (16, 16), 0)
    cj = lax.broadcasted_iota(jnp.int32, (16, 16), 1)
    before = (cj < ci).astype(BF16)
    key = route * CAPACITY
    for owner in range(OWNERS):
        mine = (route == owner).astype(F32)
        mine16 = jnp.concatenate([mine, jnp.zeros((16 - chunks, LANES), F32)], axis=0).astype(BF16)
        upto_here = jnp.dot(mine16, upto, preferred_element_type=F32)
        totals = jnp.dot(mine16, ones, preferred_element_type=F32).astype(BF16)
        offset = jnp.dot(before, totals, preferred_element_type=F32)
        rank = (upto_here + offset)[:chunks] - 1.0
        key = key + jnp.where(route == owner, rank, 0.0).astype(jnp.int32)
    square = jnp.concatenate([blend, jnp.zeros((LANES - chunks, LANES), F32)], axis=0)
    columns = square.T
    for c in range(chunks):
        weighted = rows_ref[c * LANES : (c + 1) * LANES, :] * columns[:, c : c + 1]
        high, low = halves(weighted)
        split_ref[c * LANES : (c + 1) * LANES, :LANES] = high
        split_ref[c * LANES : (c + 1) * LANES, LANES:] = low
    first, second, third = thirds(blend)
    upper = line // 32
    parts = [first, second, third, upper.astype(BF16), (line - upper * 32).astype(BF16)]
    notes = jnp.concatenate(
        [
            jnp.concatenate(
                [p.astype(F32)[c : c + 1] for p in parts] + [jnp.zeros((3, LANES), F32)], axis=0
            )
            for c in range(chunks)
        ],
        axis=1,
    ).astype(BF16)
    for step, out_ref in enumerate(out_refs):
        owner = (rep_ref[0] + step) % OWNERS
        slot = lax.broadcasted_iota(jnp.int32, (CAPACITY, LANES), 0) + owner * CAPACITY
        for c in range(chunks):
            hot = jnp.where(slot == key[c : c + 1, :], 1.0, 0.0)
            hot_ref[:, c * LANES : (c + 1) * LANES] = hot.astype(BF16)
        hot = hot_ref[...]
        both = jnp.dot(hot, split_ref[...], preferred_element_type=F32)
        out_ref[:CAPACITY, :] = both[:, :LANES] + both[:, LANES:]
        meta = lax.dot_general(
            notes, hot, (((1,), (1,)), ((), ())), preferred_element_type=F32
        )
        weight = meta[0:1] + meta[1:2] + meta[2:3]
        where = meta[3:4] * 32.0 + meta[4:5]
        out_ref[CAPACITY:, :] = jnp.concatenate(
            [weight[:, q * LANES : (q + 1) * LANES] for q in range(4)]
            + [where[:, q * LANES : (q + 1) * LANES] for q in range(4)],
            axis=0,
        )


def observe(*refs):
    got_refs, (out_ref, hot_ref) = refs[:OWNERS], refs[OWNERS:]
    total = jnp.zeros((LINES, 2 * LANES), F32)
    weights = jnp.zeros((LINES, 8), F32)
    at = lax.broadcasted_iota(jnp.int32, (LINES, LANES), 0)
    for got_ref in got_refs:
        meta = got_ref[CAPACITY:, :]
        where = meta[4:8].astype(jnp.int32)
        for q in range(4):
            hot = jnp.where(at == where[q : q + 1, :], 1.0, 0.0)
            hot_ref[:, q * LANES : (q + 1) * LANES] = hot.astype(BF16)
        hot = hot_ref[...]
        high, low = halves(got_ref[:CAPACITY, :])
        total += jnp.dot(hot, jnp.concatenate([high, low], axis=1), preferred_element_type=F32)
        weight = jnp.concatenate([meta[q : q + 1] for q in range(4)], axis=1)
        parts = [p.astype(F32) for p in thirds(weight)]
        stacked = jnp.concatenate(parts + [jnp.zeros((5, CAPACITY), F32)], axis=0).astype(BF16)
        weights += lax.dot_general(
            hot, stacked, (((1,), (1,)), ((), ())), preferred_element_type=F32
        )
    weight_sum = weights[:, 0:1] + weights[:, 1:2] + weights[:, 2:3]
    store_tiles((total[:, :LANES] + total[:, LANES:]) / weight_sum, out_ref)


def columns_from(got_ref, out_ref):
    for i in range(8):
        turned = got_ref[pl.ds(i, Z, stride=8), :].T
        for j in range(4):
            out_ref[8 * j + i] = turned[SIDE * j : SIDE * j + SIDE, :]


def store_edges(side_ref, out_ref, cross_ref, pair_ref):
    side = side_ref[0]
    cross_ref[...] = out_ref[pl.ds(side * (SIDE - RIM), RIM)]
    pair_ref[...] = out_ref[pl.ds((1 - side) * (SIDE - RIM), RIM)]


def arrive(got_ref, out_ref, swapped_ref, first_ref, last_ref, flat_ref):
    columns_from(got_ref, out_ref)
    for x in range(SIDE):
        flat_ref[SIDE * x : SIDE * x + SIDE, :] = out_ref[x]
    for y in range(SIDE):
        swapped_ref[y] = flat_ref[pl.ds(y, SIDE, stride=SIDE), :]
    first_ref[...] = swapped_ref[:RIM]
    last_ref[...] = swapped_ref[SIDE - RIM :]


def taps_of(taps_ref, flip):
    return [taps_ref[TAPS - 1 - k if flip else k] for k in range(TAPS)]


def own_share(flip, taps_ref, mid_ref, out_ref, wide_ref):
    taps = taps_of(taps_ref, flip)
    wide_ref[:8] = jnp.zeros((8, SIDE, Z), F32)
    wide_ref[8 : 8 + SIDE] = mid_ref[...]
    wide_ref[8 + SIDE :] = jnp.zeros((8, SIDE, Z), F32)

    def block(index, carry):
        row = pl.multiple_of(index * 8, 8)
        for lead in range(0, SIDE, 8):
            total = None
            for k in range(max(0, RIM - 7 - lead), min(TAPS, SIDE + RIM - lead)):
                term = taps[k] * wide_ref[lead + k - 7 : lead + k + 1, pl.ds(row, 8), :]
                total = term if total is None else total + term
            for i in range(8):
                out_ref[pl.ds(pl.multiple_of((lead + i) * SIDE + row, 8), 8), :] = total[i]
        return carry

    lax.fori_loop(0, SIDE // 8, block, 0)


def add_rims(taps_ref, flip, side, part_ref, near_ref, far_ref, edge_ref, flat_ref):
    taps = taps_of(taps_ref, flip)
    zeros = jnp.zeros((8, SIDE, Z), F32)
    edge_ref[0, RIM : RIM + 8] = zeros
    edge_ref[1, :8] = zeros
    edge_ref[side, pl.ds(8 * side, RIM)] = near_ref[...]
    edge_ref[1 - side, pl.ds(8 * (1 - side), RIM)] = far_ref[...]

    def block(index, carry):
        row = pl.multiple_of(index * 8, 8)
        for lead in range(0, SIDE, 8):
            if lead < SIDE // 2:
                side, first, ks = 0, lead, range(0, RIM - lead)
            else:
                side, first, ks = 1, lead - 39, range(SIDE + RIM - 7 - lead, TAPS)
            spots = [pl.ds(pl.multiple_of((lead + i) * SIDE + row, 8), 8) for i in range(8)]
            total = None
            for k in ks:
                term = taps[k] * edge_ref[side, first + k : first + k + 8, pl.ds(row, 8), :]
                total = term if total is None else total + term
            for i in range(8):
                flat_ref[spots[i], :] = part_ref[spots[i], :] + total[i]
        return carry

    lax.fori_loop(0, SIDE // 8, block, 0)


def along_x(
    flip, taps_ref, side_ref, part_ref, cross_ref, pair_ref, out_ref, first_ref, last_ref, edge_ref, flat_ref
):
    add_rims(taps_ref, flip, side_ref[0], part_ref, cross_ref, pair_ref, edge_ref, flat_ref)
    for y in range(SIDE):
        out_ref[y] = flat_ref[pl.ds(y, SIDE, stride=SIDE), :]
    first_ref[...] = out_ref[:RIM]
    last_ref[...] = out_ref[SIDE - RIM :]


def along_y(taps_ref, flip, part_ref, low_ref, high_ref, edge_ref, flat_ref, out_ref):
    add_rims(taps_ref, flip, 0, part_ref, low_ref, high_ref, edge_ref, flat_ref)
    for x in range(SIDE):
        out_ref[SIDE * x : SIDE * x + SIDE, :] = flat_ref[pl.ds(x, SIDE, stride=SIDE), :]


def axial(value, band, back):
    return lax.dot_general(
        value,
        band,
        (((1,), (0 if back else 1,)), ((), ())),
        precision=lax.Precision.HIGHEST,
        preferred_element_type=F32,
    )


def along_y_first(
    taps_ref, side_ref, part_ref, low_ref, high_ref, out_ref, cross_ref, pair_ref, edge_ref, flat_ref, cols_ref
):
    along_y(taps_ref, False, part_ref, low_ref, high_ref, edge_ref, flat_ref, cols_ref)
    out_ref[...] = cols_ref[...].reshape(SIDE, SIDE, Z)
    store_edges(side_ref, out_ref, cross_ref, pair_ref)


def blur_x_last(taps_ref, side_ref, part_ref, cross_ref, pair_ref, band_ref, out_ref, edge_ref, flat_ref):
    add_rims(taps_ref, False, side_ref[0], part_ref, cross_ref, pair_ref, edge_ref, flat_ref)
    out_ref[...] = axial(flat_ref[...], band_ref[...], False)


def back_axial(side_ref, ratio, band_ref, out_ref, cross_ref, pair_ref):
    out_ref[...] = axial(ratio, band_ref[...], True).reshape(SIDE, SIDE, Z)
    store_edges(side_ref, out_ref, cross_ref, pair_ref)


def first_ratio(side_ref, got_ref, blurred_ref, band_ref, seen_ref, out_ref, cross_ref, pair_ref):
    columns_from(got_ref, seen_ref)
    ratio = seen_ref[...].reshape(SIDE * SIDE, Z) / blurred_ref[...]
    back_axial(side_ref, ratio, band_ref, out_ref, cross_ref, pair_ref)


def blur_ratio(
    taps_ref,
    side_ref,
    part_ref,
    low_ref,
    high_ref,
    band_ref,
    seen_ref,
    out_ref,
    cross_ref,
    pair_ref,
    edge_ref,
    flat_ref,
    cols_ref,
):
    along_y(taps_ref, False, part_ref, low_ref, high_ref, edge_ref, flat_ref, cols_ref)
    blurred = axial(cols_ref[...], band_ref[...], False)
    ratio = seen_ref[...].reshape(SIDE * SIDE, Z) / blurred
    back_axial(side_ref, ratio, band_ref, out_ref, cross_ref, pair_ref)


def update(
    taps_ref,
    side_ref,
    part_ref,
    low_ref,
    high_ref,
    estimate_ref,
    out_ref,
    cross_ref,
    pair_ref,
    edge_ref,
    flat_ref,
    cols_ref,
):
    along_y(taps_ref, True, part_ref, low_ref, high_ref, edge_ref, flat_ref, cols_ref)
    out_ref[...] = estimate_ref[...] * cols_ref[...].reshape(SIDE, SIDE, Z)
    store_edges(side_ref, out_ref, cross_ref, pair_ref)


def last_update(
    taps_ref, part_ref, low_ref, high_ref, estimate_ref, out_ref, edge_ref, flat_ref, cols_ref
):
    along_y(taps_ref, True, part_ref, low_ref, high_ref, edge_ref, flat_ref, cols_ref)
    for i in range(8):
        block = jnp.concatenate(
            [
                estimate_ref[8 * j + i] * cols_ref[SIDE * (8 * j + i) : SIDE * (8 * j + i) + SIDE, :]
                for j in range(4)
            ],
            axis=0,
        )
        out_ref[pl.ds(i, Z, stride=8), :] = block.T


def plane_of(got_ref, out_ref):
    outs = lane_blocks([got_ref[32 * sub : 32 * sub + 32] for sub in range(4)])
    for j, out in enumerate(outs):
        out_ref[:, 8 * j : 8 * j + 8, :] = out


TILE = (SIDE, SIDE, Z)
EDGE = (RIM, SIDE, Z)
PIECES = (Z, 8, LANES)
FLAT = (SIDE * SIDE, Z)
SCRATCH = [((2, RIM + 8, SIDE, Z), F32), (FLAT, F32), (FLAT, F32)]
WIDE = [((SIDE + 16, SIDE, Z), F32)]


def shards(camera_rows, blend, route, line, start, psf_xy, psf_z):
    slabs, reps = lax.axis_size("slab"), lax.axis_size("rep")
    x_tiles = LINES // SIDE
    y_tiles = slabs // x_tiles
    chunks = camera_rows.shape[0] // LANES
    pair_swaps = [(t, t ^ 1) for t in range(slabs)]
    cross_swaps = []
    for t in range(1, slabs, 2):
        if t % x_tiles != x_tiles - 1:
            cross_swaps += [(t, t + 1), (t + 1, t)]
    side = (lax.axis_index("slab") % 2).reshape(1)
    y_pairs = []
    for t in range(slabs):
        for r in range(reps):
            y = r * y_tiles + t // x_tiles + 1
            if y < y_tiles * reps:
                up = (y % y_tiles) * x_tiles + t % x_tiles
                y_pairs.append((t * reps + r, up * reps + y // y_tiles))

    def rims_x(cross, pair):
        return lax.ppermute(cross, "slab", cross_swaps), lax.ppermute(pair, "slab", pair_swaps)

    def rims_y(first, last):
        axes = ("slab", "rep")
        return lax.ppermute(last, axes, y_pairs), lax.ppermute(first, axes, [(b, a) for a, b in y_pairs])

    def turn(pieces):
        return lax.all_to_all(pieces, "slab", split_axis=0, concat_axis=0, tiled=True)

    taps = psf_xy / jnp.sum(psf_xy)

    arrived = turn(call(tiles_of_start, [PIECES], [], start.reshape(LINES, LANES))[0])
    band = call(axial_band, [(Z, LANES)], [((8, LANES), F32)], psf_z[None, :])[0]
    sent = call(
        pack_rows,
        [(CAPACITY + META, LANES)] * OWNERS,
        [((chunks * LANES, 2 * LANES), BF16), ((CAPACITY, chunks * LANES), BF16)],
        lax.axis_index("rep").reshape(1),
        camera_rows,
        blend.reshape(chunks, LANES),
        route.reshape(chunks, LANES),
        line.reshape(chunks, LANES),
        smem=1,
    )
    got = [
        block if step == 0 else lax.ppermute(block, "rep", [(r, (r + step) % reps) for r in range(reps)])
        for step, block in enumerate(sent)
    ]
    seen_pieces = call(observe, [PIECES], [((LINES, CAPACITY), BF16)], *got)[0]
    arrived, seen_pieces = lax.optimization_barrier((arrived, seen_pieces))
    estimate, swapped, first, last = call(
        arrive, [TILE, TILE, EDGE, EDGE], SCRATCH[1:2], arrived.reshape(Z * 8, LANES)
    )
    seen_arrived = turn(seen_pieces)
    own = functools.partial(call, functools.partial(own_share, False), [FLAT], WIDE, taps, smem=1)
    own_back = functools.partial(call, functools.partial(own_share, True), [FLAT], WIDE, taps, smem=1)

    def lateral(flip, part, rims):
        value, first, last = call(
            functools.partial(along_x, flip), [TILE, EDGE, EDGE], SCRATCH[:2], taps, side, part, *rims, smem=2
        )
        rims = rims_y(first, last)
        return (own_back if flip else own)(value)[0], *rims

    value, *edges = call(
        along_y_first, [TILE, EDGE, EDGE], SCRATCH, taps, side, own(swapped)[0], *rims_y(first, last), smem=2
    )
    blurred = call(
        blur_x_last, [FLAT], SCRATCH[:2], taps, side, own(value)[0], *rims_x(*edges), band, smem=2
    )[0]
    seen, back, *edges = call(
        first_ratio, [TILE, TILE, EDGE, EDGE], [], side, seen_arrived.reshape(Z * 8, LANES), blurred, band, smem=1
    )
    parts = lateral(True, own_back(back)[0], rims_x(*edges))
    estimate, *edges = call(
        update, [TILE, EDGE, EDGE], SCRATCH, taps, side, *parts, estimate, smem=2
    )
    parts = lateral(False, own(estimate)[0], rims_x(*edges))
    back, *edges = call(
        blur_ratio, [TILE, EDGE, EDGE], SCRATCH, taps, side, *parts, band, seen, smem=2
    )
    parts = lateral(True, own_back(back)[0], rims_x(*edges))
    pieces = call(last_update, [(Z * 8, LANES)], SCRATCH, taps, *parts, estimate, smem=1)[0]
    done = turn(pieces.reshape(PIECES))
    plane = call(plane_of, [(LINES // SIDE, SIDE, LANES)], [], done)[0]
    return plane.reshape(1, LINES, LANES)


def solution(mesh):
    in_specs = (
        P(("slab", "rep"), None),
        P(("slab", "rep")),
        P(("slab", "rep")),
        P(("slab", "rep")),
        P("slab", None, "rep"),
        P(),
        P(),
    )
    out_specs = P("slab", None, "rep")
    return jax.shard_map(shards, mesh=mesh, in_specs=in_specs, out_specs=out_specs, check_vma=False)
```

```python
import functools

import jax
import jax.numpy as jnp
from jax import lax
from jax.experimental import pallas as pl
from jax.experimental.pallas import tpu as pltpu
from jax.sharding import PartitionSpec as P

F32 = jnp.float32
BF16 = jnp.bfloat16
LANES = 128
SIDE = 32
TAPS = 31
RIM = TAPS // 2
OWNERS = 4
CAPACITY = 512
META = 8
LINES = 1024
Z = 128
VMEM_LIMIT = 40 * 1024 * 1024


def call(kernel, out_shapes, scratch, *args, smem=0):
    specs = [
        pl.BlockSpec(memory_space=pltpu.SMEM if i < smem else pltpu.VMEM)
        for i in range(len(args))
    ]
    outs = tuple(jax.ShapeDtypeStruct(s, F32) for s in out_shapes)
    return pl.pallas_call(
        kernel,
        out_shape=outs,
        in_specs=specs,
        out_specs=tuple(pl.BlockSpec(memory_space=pltpu.VMEM) for _ in outs),
        scratch_shapes=[pltpu.VMEM(s, d) for s, d in scratch],
        compiler_params=pltpu.CompilerParams(vmem_limit_bytes=VMEM_LIMIT),
        name=kernel.func.__name__ if isinstance(kernel, functools.partial) else kernel.__name__,
    )(*args)


def halves(value):
    high = value.astype(BF16)
    return high, (value - high.astype(F32)).astype(BF16)


def thirds(value):
    high, rest = halves(value)
    low = (value - high.astype(F32) - rest.astype(F32)).astype(BF16)
    return high, rest, low


def swap_lanes(pairs, first, moves):
    mixed = [jnp.where(first, b, a) for a, b in pairs]
    up = [pltpu.roll(m, moves[0], axis=1) for m in mixed]
    down = up if moves[0] == moves[1] else [pltpu.roll(m, moves[1], axis=1) for m in mixed]
    return [
        (jnp.where(first, a, u), jnp.where(first, d, b)) for (a, b), u, d in zip(pairs, up, down, strict=True)
    ]


def lane_blocks(pieces):
    lane = lax.broadcasted_iota(jnp.int32, (8, LANES), 1)
    outer = swap_lanes([pair for a, b, c, d in pieces for pair in ((a, c), (b, d))], lane < 64, (64, 64))
    rows = [(ac[0], bd[0], ac[1], bd[1]) for ac, bd in zip(outer[::2], outer[1::2], strict=True)]
    inner = swap_lanes([pair for a, b, c, d in rows for pair in ((a, b), (c, d))], lane % 64 < 32, (32, 96))
    return [ab + cd for ab, cd in zip(inner[::2], inner[1::2], strict=True)]


def store_tiles(plane_ref, out_ref):
    for first in range(0, 32, 8):
        parts = range(first, first + 8)
        rows = [
            tuple(plane_ref[SIDE * p + 8 * j : SIDE * p + 8 * j + 8, :] for j in range(4)) for p in parts
        ]
        for part, piece in zip(parts, lane_blocks(rows), strict=True):
            for sub in range(4):
                out_ref[32 * sub + part] = piece[sub]


def plane_of(got_ref, out_ref):
    for first in range(0, 32, 8):
        parts = range(first, first + 8)
        pieces = [tuple(got_ref[32 * sub + p] for sub in range(4)) for p in parts]
        for part, rows in zip(parts, lane_blocks(pieces), strict=True):
            for j in range(4):
                out_ref[SIDE * part + 8 * j : SIDE * part + 8 * j + 8, :] = rows[j]


def axial_band(psf_ref, out_ref, row_ref):
    row_ref[...] = jnp.zeros((8, LANES), F32)
    row_ref[0:1, : psf_ref.shape[1]] = psf_ref[...]
    psf = row_ref[0:1, :]
    rows = jnp.broadcast_to(psf / jnp.sum(psf, axis=1, keepdims=True), (Z, LANES))
    rolled = pltpu.roll(rows, LANES - 31, axis=1, stride=1, stride_axis=0)
    a = lax.broadcasted_iota(jnp.int32, (Z, LANES), 0)
    b = lax.broadcasted_iota(jnp.int32, (Z, LANES), 1)
    out_ref[...] = jnp.where(jnp.abs(a - b) <= 31, rolled, 0.0)


def pack_rows(rep_ref, rows_ref, blend_ref, route_ref, line_ref, *refs):
    out_refs, (split_ref, hot_ref) = refs[:OWNERS], refs[OWNERS:]
    chunks = rows_ref.shape[0] // LANES
    blend = blend_ref[...]
    route = route_ref[...]
    line = line_ref[...]
    i = lax.broadcasted_iota(jnp.int32, (LANES, LANES), 0)
    j = lax.broadcasted_iota(jnp.int32, (LANES, LANES), 1)
    upto = (i <= j).astype(BF16)
    ones = jnp.ones((LANES, LANES), BF16)
    ci = lax.broadcasted_iota(jnp.int32, (16, 16), 0)
    cj = lax.broadcasted_iota(jnp.int32, (16, 16), 1)
    before = (cj < ci).astype(BF16)
    key = route * CAPACITY
    for owner in range(OWNERS):
        mine = (route == owner).astype(F32)
        mine16 = jnp.concatenate([mine, jnp.zeros((16 - chunks, LANES), F32)], axis=0).astype(BF16)
        upto_here = jnp.dot(mine16, upto, preferred_element_type=F32)
        totals = jnp.dot(mine16, ones, preferred_element_type=F32).astype(BF16)
        offset = jnp.dot(before, totals, preferred_element_type=F32)
        rank = (upto_here + offset)[:chunks] - 1.0
        key = key + jnp.where(route == owner, rank, 0.0).astype(jnp.int32)
    square = jnp.concatenate([blend, jnp.zeros((LANES - chunks, LANES), F32)], axis=0)
    columns = square.T
    for c in range(chunks):
        weighted = rows_ref[c * LANES : (c + 1) * LANES, :] * columns[:, c : c + 1]
        high, low = halves(weighted)
        split_ref[c * LANES : (c + 1) * LANES, :LANES] = high
        split_ref[c * LANES : (c + 1) * LANES, LANES:] = low
    first, second, third = thirds(blend)
    upper = line // 32
    parts = [first, second, third, upper.astype(BF16), (line - upper * 32).astype(BF16)]
    notes = jnp.concatenate(
        [
            jnp.concatenate(
                [p.astype(F32)[c : c + 1] for p in parts] + [jnp.zeros((3, LANES), F32)], axis=0
            )
            for c in range(chunks)
        ],
        axis=1,
    ).astype(BF16)
    for step, out_ref in enumerate(out_refs):
        owner = (rep_ref[0] + step) % OWNERS
        slot = lax.broadcasted_iota(jnp.int32, (CAPACITY, LANES), 0) + owner * CAPACITY
        for c in range(chunks):
            hot = jnp.where(slot == key[c : c + 1, :], 1.0, 0.0)
            hot_ref[:, c * LANES : (c + 1) * LANES] = hot.astype(BF16)
        hot = hot_ref[...]
        both = jnp.dot(hot, split_ref[...], preferred_element_type=F32)
        out_ref[:CAPACITY, :] = both[:, :LANES] + both[:, LANES:]
        meta = lax.dot_general(
            notes, hot, (((1,), (1,)), ((), ())), preferred_element_type=F32
        )
        weight = meta[0:1] + meta[1:2] + meta[2:3]
        where = meta[3:4] * 32.0 + meta[4:5]
        out_ref[CAPACITY:, :] = jnp.concatenate(
            [weight[:, q * LANES : (q + 1) * LANES] for q in range(4)]
            + [where[:, q * LANES : (q + 1) * LANES] for q in range(4)],
            axis=0,
        )


def observe(*refs):
    got_refs, (out_ref, hot_ref, plane_ref) = refs[:OWNERS], refs[OWNERS:]
    total = jnp.zeros((LINES, 2 * LANES), F32)
    weights = jnp.zeros((LINES, 8), F32)
    at = lax.broadcasted_iota(jnp.int32, (LINES, LANES), 0)
    for got_ref in got_refs:
        meta = got_ref[CAPACITY:, :]
        where = meta[4:8].astype(jnp.int32)
        for q in range(4):
            hot = jnp.where(at == where[q : q + 1, :], 1.0, 0.0)
            hot_ref[:, q * LANES : (q + 1) * LANES] = hot.astype(BF16)
        hot = hot_ref[...]
        high, low = halves(got_ref[:CAPACITY, :])
        total += jnp.dot(hot, jnp.concatenate([high, low], axis=1), preferred_element_type=F32)
        weight = jnp.concatenate([meta[q : q + 1] for q in range(4)], axis=1)
        parts = [p.astype(F32) for p in thirds(weight)]
        stacked = jnp.concatenate(parts + [jnp.zeros((5, CAPACITY), F32)], axis=0).astype(BF16)
        weights += lax.dot_general(
            hot, stacked, (((1,), (1,)), ((), ())), preferred_element_type=F32
        )
    weight_sum = weights[:, 0:1] + weights[:, 1:2] + weights[:, 2:3]
    plane_ref[...] = (total[:, :LANES] + total[:, LANES:]) / weight_sum
    store_tiles(plane_ref, out_ref)


def columns_from(got_ref, out_ref):
    for i in range(8):
        turned = got_ref[pl.ds(i, Z, stride=8), :].T
        for j in range(4):
            out_ref[SIDE * (8 * j + i) : SIDE * (8 * j + i) + SIDE, :] = turned[SIDE * j : SIDE * j + SIDE, :]


def store_ends(out_ref, first_ref, last_ref):
    first_ref[...] = out_ref[: RIM * SIDE, :]
    last_ref[...] = out_ref[(SIDE - RIM) * SIDE :, :]


def store_edges(side_ref, out_ref, cross_ref, pair_ref):
    skip = (SIDE - RIM) * SIDE
    cross_ref[...] = out_ref[pl.ds(pl.multiple_of(side_ref[0] * skip, 8), RIM * SIDE), :]
    pair_ref[...] = out_ref[pl.ds(pl.multiple_of((1 - side_ref[0]) * skip, 8), RIM * SIDE), :]


def arrive(got_ref, out_ref, swapped_ref, first_ref, last_ref):
    columns_from(got_ref, out_ref)
    for y in range(SIDE):
        swapped_ref[SIDE * y : SIDE * y + SIDE, :] = out_ref[pl.ds(y, SIDE, stride=SIDE), :]
    store_ends(swapped_ref, first_ref, last_ref)


def taps_of(taps_ref, flip):
    return [taps_ref[TAPS - 1 - k if flip else k] for k in range(TAPS)]


def own_share(flip, taps_ref, mid_ref, out_ref):
    taps = taps_of(taps_ref, flip)

    def block(index, carry):
        row = index * 8
        for lead in range(0, SIDE, 8):
            totals = [None] * 8
            for cell in range(max(0, lead - RIM), min(SIDE, lead + 8 + RIM)):
                value = mid_ref[pl.ds(pl.multiple_of(cell * SIDE + row, 8), 8), :]
                for i in range(8):
                    k = cell - lead - i + RIM
                    if 0 <= k < TAPS:
                        term = taps[k] * value
                        totals[i] = term if totals[i] is None else totals[i] + term
            for i in range(8):
                out_ref[pl.ds(pl.multiple_of((lead + i) * SIDE + row, 8), 8), :] = totals[i]
        return carry

    lax.fori_loop(0, SIDE // 8, block, 0)


def add_rims(taps_ref, flip, side, part_ref, near_ref, far_ref, store):
    taps = taps_of(taps_ref, flip)
    for row in range(0, SIDE, 8):
        near = [near_ref[SIDE * i + row : SIDE * i + row + 8, :] for i in range(RIM)]
        far = [far_ref[SIDE * i + row : SIDE * i + row + 8, :] for i in range(RIM)]
        if side is None:
            low, high = near, far
        else:
            low = [jnp.where(side == 0, a, b) for a, b in zip(near, far, strict=True)]
            high = [jnp.where(side == 0, b, a) for a, b in zip(near, far, strict=True)]
        for lead in range(SIDE):
            total = part_ref[SIDE * lead + row : SIDE * lead + row + 8, :]
            for i in range(RIM):
                if i >= lead:
                    total = total + taps[i - lead] * low[i]
                if i <= lead - SIDE + RIM:
                    total = total + taps[SIDE + RIM + i - lead] * high[i]
            store(lead, row, total)


def swapped(lead, row):
    return pl.ds(SIDE * row + lead, 8, stride=SIDE)


def along_x(flip, taps_ref, side_ref, part_ref, cross_ref, pair_ref, out_ref, first_ref, last_ref):
    def store(lead, row, value):
        out_ref[swapped(lead, row), :] = value

    add_rims(taps_ref, flip, side_ref[0], part_ref, cross_ref, pair_ref, store)
    store_ends(out_ref, first_ref, last_ref)


def along_y_first(taps_ref, side_ref, part_ref, low_ref, high_ref, out_ref, cross_ref, pair_ref):
    def store(lead, row, value):
        out_ref[swapped(lead, row), :] = value

    add_rims(taps_ref, False, None, part_ref, low_ref, high_ref, store)
    store_edges(side_ref, out_ref, cross_ref, pair_ref)


def axial(value, band, back):
    dims = (((1,), (0 if back else 1,)), ((), ()))
    high, low = halves(value)
    band_high, band_low = halves(band)
    double = jnp.concatenate([band_high, band_high], axis=0 if back else 1)
    both = jnp.concatenate([high, low], axis=1)
    return lax.dot_general(both, double, dims, preferred_element_type=F32) + lax.dot_general(
        high, band_low, dims, preferred_element_type=F32
    )


def blur_x_last(taps_ref, side_ref, part_ref, cross_ref, pair_ref, band_ref, out_ref, cols_ref):
    def store(lead, row, value):
        cols_ref[SIDE * lead + row : SIDE * lead + row + 8, :] = value

    add_rims(taps_ref, False, side_ref[0], part_ref, cross_ref, pair_ref, store)
    out_ref[...] = axial(cols_ref[...], band_ref[...], False)


def first_ratio(side_ref, got_ref, blurred_ref, band_ref, seen_ref, out_ref, cross_ref, pair_ref):
    columns_from(got_ref, seen_ref)
    out_ref[...] = axial(seen_ref[...] / blurred_ref[...], band_ref[...], True)
    store_edges(side_ref, out_ref, cross_ref, pair_ref)


def blur_ratio(
    taps_ref, side_ref, part_ref, low_ref, high_ref, band_ref, seen_ref, out_ref, cross_ref, pair_ref, cols_ref
):
    def store(lead, row, value):
        cols_ref[swapped(lead, row), :] = value

    add_rims(taps_ref, False, None, part_ref, low_ref, high_ref, store)
    band = band_ref[...]
    for start in range(0, SIDE * SIDE, 256):
        spot = slice(start, start + 256)
        ratio = seen_ref[spot, :] / axial(cols_ref[spot, :], band, False)
        out_ref[spot, :] = axial(ratio, band, True)
    store_edges(side_ref, out_ref, cross_ref, pair_ref)


def update(taps_ref, side_ref, part_ref, low_ref, high_ref, estimate_ref, out_ref, cross_ref, pair_ref):
    def store(lead, row, value):
        spot = swapped(lead, row)
        out_ref[spot, :] = estimate_ref[spot, :] * value

    add_rims(taps_ref, True, None, part_ref, low_ref, high_ref, store)
    store_edges(side_ref, out_ref, cross_ref, pair_ref)


def last_update(taps_ref, part_ref, low_ref, high_ref, estimate_ref, out_ref, cols_ref):
    def store(lead, row, value):
        cols_ref[swapped(lead, row), :] = value

    add_rims(taps_ref, True, None, part_ref, low_ref, high_ref, store)
    for i in range(8):
        spots = [slice(SIDE * (8 * j + i), SIDE * (8 * j + i) + SIDE) for j in range(4)]
        block = jnp.concatenate([estimate_ref[spot, :] * cols_ref[spot, :] for spot in spots], axis=0)
        out_ref[pl.ds(i, Z, stride=8), :] = block.T


FLAT = (SIDE * SIDE, Z)
EDGE = (RIM * SIDE, Z)
PIECES = (Z, 8, LANES)


def shards(camera_rows, blend, route, line, start, psf_xy, psf_z):
    slabs, reps = lax.axis_size("slab"), lax.axis_size("rep")
    x_tiles = LINES // SIDE
    y_tiles = slabs // x_tiles
    chunks = camera_rows.shape[0] // LANES
    pair_swaps = [(t, t ^ 1) for t in range(slabs)]
    cross_swaps = []
    for t in range(1, slabs, 2):
        if t % x_tiles != x_tiles - 1:
            cross_swaps += [(t, t + 1), (t + 1, t)]
    side = (lax.axis_index("slab") % 2).reshape(1)
    y_pairs = []
    for t in range(slabs):
        for r in range(reps):
            y = r * y_tiles + t // x_tiles + 1
            if y < y_tiles * reps:
                up = (y % y_tiles) * x_tiles + t % x_tiles
                y_pairs.append((t * reps + r, up * reps + y // y_tiles))

    def rims_x(cross, pair):
        return lax.ppermute(cross, "slab", cross_swaps), lax.ppermute(pair, "slab", pair_swaps)

    def rims_y(first, last):
        axes = ("slab", "rep")
        return lax.ppermute(last, axes, y_pairs), lax.ppermute(first, axes, [(b, a) for a, b in y_pairs])

    def turn(pieces):
        return lax.all_to_all(pieces, "slab", split_axis=0, concat_axis=0, tiled=True)

    taps = psf_xy / jnp.sum(psf_xy)

    arrived = turn(call(store_tiles, [PIECES], [], start.reshape(LINES, LANES))[0])
    band = call(axial_band, [(Z, LANES)], [((8, LANES), F32)], psf_z[None, :])[0]
    sent = call(
        pack_rows,
        [(CAPACITY + META, LANES)] * OWNERS,
        [((chunks * LANES, 2 * LANES), BF16), ((CAPACITY, chunks * LANES), BF16)],
        lax.axis_index("rep").reshape(1),
        camera_rows,
        blend.reshape(chunks, LANES),
        route.reshape(chunks, LANES),
        line.reshape(chunks, LANES),
        smem=1,
    )
    got = [
        block if step == 0 else lax.ppermute(block, "rep", [(r, (r + step) % reps) for r in range(reps)])
        for step, block in enumerate(sent)
    ]
    seen_pieces = call(observe, [PIECES], [((LINES, CAPACITY), BF16), ((LINES, LANES), F32)], *got)[0]
    arrived, seen_pieces = lax.optimization_barrier((arrived, seen_pieces))
    estimate, flipped, first, last = call(
        arrive, [FLAT, FLAT, EDGE, EDGE], [], arrived.reshape(Z * 8, LANES)
    )
    seen_arrived = turn(seen_pieces)
    own = functools.partial(call, functools.partial(own_share, False), [FLAT], [], taps, smem=1)
    own_back = functools.partial(call, functools.partial(own_share, True), [FLAT], [], taps, smem=1)

    def lateral(flip, part, rims):
        value, first, last = call(
            functools.partial(along_x, flip), [FLAT, EDGE, EDGE], [], taps, side, part, *rims, smem=2
        )
        rims = rims_y(first, last)
        return (own_back if flip else own)(value)[0], *rims

    value, *edges = call(
        along_y_first, [FLAT, EDGE, EDGE], [], taps, side, own(flipped)[0], *rims_y(first, last), smem=2
    )
    cols = [(FLAT, F32)]
    blurred = call(
        blur_x_last, [FLAT], cols, taps, side, own(value)[0], *rims_x(*edges), band, smem=2
    )[0]
    seen, back, *edges = call(
        first_ratio, [FLAT, FLAT, EDGE, EDGE], [], side, seen_arrived.reshape(Z * 8, LANES), blurred, band, smem=1
    )
    parts = lateral(True, own_back(back)[0], rims_x(*edges))
    estimate, *edges = call(update, [FLAT, EDGE, EDGE], [], taps, side, *parts, estimate, smem=2)
    parts = lateral(False, own(estimate)[0], rims_x(*edges))
    back, *edges = call(
        blur_ratio, [FLAT, EDGE, EDGE], cols, taps, side, *parts, band, seen, smem=2
    )
    parts = lateral(True, own_back(back)[0], rims_x(*edges))
    pieces = call(last_update, [(Z * 8, LANES)], cols, taps, *parts, estimate, smem=1)[0]
    done = turn(pieces.reshape(PIECES))
    plane = call(plane_of, [(LINES, LANES)], [], done)[0]
    return plane.reshape(1, LINES, LANES)


def solution(mesh):
    in_specs = (
        P(("slab", "rep"), None),
        P(("slab", "rep")),
        P(("slab", "rep")),
        P(("slab", "rep")),
        P("slab", None, "rep"),
        P(),
        P(),
    )
    out_specs = P("slab", None, "rep")
    return jax.shard_map(shards, mesh=mesh, in_specs=in_specs, out_specs=out_specs, check_vma=False)
```

```python
import functools

import jax
import jax.numpy as jnp
from jax import lax
from jax.experimental import pallas as pl
from jax.experimental.pallas import tpu as pltpu
from jax.sharding import PartitionSpec as P

F32 = jnp.float32
BF16 = jnp.bfloat16
LANES = 128
SIDE = 32
TAPS = 31
RIM = TAPS // 2
WIDE = 64
MARGIN = 16
OWNERS = 4
CAPACITY = 512
META = 8
LINES = 1024
Z = 128
VMEM_LIMIT = 40 * 1024 * 1024


def call(kernel, out_shapes, scratch, *args, smem=0):
    specs = [
        pl.BlockSpec(memory_space=pltpu.SMEM if i < smem else pltpu.VMEM)
        for i in range(len(args))
    ]
    outs = tuple(jax.ShapeDtypeStruct(s, F32) for s in out_shapes)
    return pl.pallas_call(
        kernel,
        out_shape=outs,
        in_specs=specs,
        out_specs=tuple(pl.BlockSpec(memory_space=pltpu.VMEM) for _ in outs),
        scratch_shapes=[pltpu.VMEM(s, d) for s, d in scratch],
        compiler_params=pltpu.CompilerParams(vmem_limit_bytes=VMEM_LIMIT),
        name=kernel.func.__name__ if isinstance(kernel, functools.partial) else kernel.__name__,
    )(*args)


def halves(value):
    high = value.astype(BF16)
    return high, (value - high.astype(F32)).astype(BF16)


def thirds(value):
    high, rest = halves(value)
    low = (value - high.astype(F32) - rest.astype(F32)).astype(BF16)
    return high, rest, low


def swap_lanes(pairs, first, moves):
    mixed = [jnp.where(first, b, a) for a, b in pairs]
    up = [pltpu.roll(m, moves[0], axis=1) for m in mixed]
    down = up if moves[0] == moves[1] else [pltpu.roll(m, moves[1], axis=1) for m in mixed]
    return [
        (jnp.where(first, a, u), jnp.where(first, d, b)) for (a, b), u, d in zip(pairs, up, down, strict=True)
    ]


def lane_blocks(pieces):
    lane = lax.broadcasted_iota(jnp.int32, (8, LANES), 1)
    outer = swap_lanes([pair for a, b, c, d in pieces for pair in ((a, c), (b, d))], lane < 64, (64, 64))
    rows = [(ac[0], bd[0], ac[1], bd[1]) for ac, bd in zip(outer[::2], outer[1::2], strict=True)]
    inner = swap_lanes([pair for a, b, c, d in rows for pair in ((a, b), (c, d))], lane % 64 < 32, (32, 96))
    return [ab + cd for ab, cd in zip(inner[::2], inner[1::2], strict=True)]


def store_tiles(plane_ref, out_ref):
    for first in range(0, 32, 8):
        parts = range(first, first + 8)
        rows = [
            tuple(plane_ref[SIDE * p + 8 * j : SIDE * p + 8 * j + 8, :] for j in range(4)) for p in parts
        ]
        for part, piece in zip(parts, lane_blocks(rows), strict=True):
            for sub in range(4):
                out_ref[32 * sub + part] = piece[sub]


def plane_of(got_ref, out_ref):
    for first in range(0, 32, 8):
        parts = range(first, first + 8)
        pieces = [tuple(got_ref[32 * sub + p] for sub in range(4)) for p in parts]
        for part, rows in zip(parts, lane_blocks(pieces), strict=True):
            for j in range(4):
                out_ref[SIDE * part + 8 * j : SIDE * part + 8 * j + 8, :] = rows[j]


def axial_band(psf_ref, out_ref, row_ref):
    row_ref[...] = jnp.zeros((8, LANES), F32)
    row_ref[0:1, : psf_ref.shape[1]] = psf_ref[...]
    psf = row_ref[0:1, :]
    rows = jnp.broadcast_to(psf / jnp.sum(psf, axis=1, keepdims=True), (Z, LANES))
    rolled = pltpu.roll(rows, LANES - 31, axis=1, stride=1, stride_axis=0)
    a = lax.broadcasted_iota(jnp.int32, (Z, LANES), 0)
    b = lax.broadcasted_iota(jnp.int32, (Z, LANES), 1)
    out_ref[...] = jnp.where(jnp.abs(a - b) <= 31, rolled, 0.0)


def pack_rows(rep_ref, rows_ref, blend_ref, route_ref, line_ref, *refs):
    out_refs, (split_ref, hot_ref) = refs[:OWNERS], refs[OWNERS:]
    chunks = rows_ref.shape[0] // LANES
    blend = blend_ref[...]
    route = route_ref[...]
    line = line_ref[...]
    i = lax.broadcasted_iota(jnp.int32, (LANES, LANES), 0)
    j = lax.broadcasted_iota(jnp.int32, (LANES, LANES), 1)
    upto = (i <= j).astype(BF16)
    ones = jnp.ones((LANES, LANES), BF16)
    ci = lax.broadcasted_iota(jnp.int32, (16, 16), 0)
    cj = lax.broadcasted_iota(jnp.int32, (16, 16), 1)
    before = (cj < ci).astype(BF16)
    key = route * CAPACITY
    for owner in range(OWNERS):
        mine = (route == owner).astype(F32)
        mine16 = jnp.concatenate([mine, jnp.zeros((16 - chunks, LANES), F32)], axis=0).astype(BF16)
        upto_here = jnp.dot(mine16, upto, preferred_element_type=F32)
        totals = jnp.dot(mine16, ones, preferred_element_type=F32).astype(BF16)
        offset = jnp.dot(before, totals, preferred_element_type=F32)
        rank = (upto_here + offset)[:chunks] - 1.0
        key = key + jnp.where(route == owner, rank, 0.0).astype(jnp.int32)
    square = jnp.concatenate([blend, jnp.zeros((LANES - chunks, LANES), F32)], axis=0)
    columns = square.T
    for c in range(chunks):
        weighted = rows_ref[c * LANES : (c + 1) * LANES, :] * columns[:, c : c + 1]
        high, low = halves(weighted)
        split_ref[c * LANES : (c + 1) * LANES, :LANES] = high
        split_ref[c * LANES : (c + 1) * LANES, LANES:] = low
    first, second, third = thirds(blend)
    upper = line // 32
    parts = [first, second, third, upper.astype(BF16), (line - upper * 32).astype(BF16)]
    notes = jnp.concatenate(
        [
            jnp.concatenate(
                [p.astype(F32)[c : c + 1] for p in parts] + [jnp.zeros((3, LANES), F32)], axis=0
            )
            for c in range(chunks)
        ],
        axis=1,
    ).astype(BF16)
    for step, out_ref in enumerate(out_refs):
        owner = (rep_ref[0] + step) % OWNERS
        slot = lax.broadcasted_iota(jnp.int32, (CAPACITY, LANES), 0) + owner * CAPACITY
        for c in range(chunks):
            hot = jnp.where(slot == key[c : c + 1, :], 1.0, 0.0)
            hot_ref[:, c * LANES : (c + 1) * LANES] = hot.astype(BF16)
        hot = hot_ref[...]
        both = jnp.dot(hot, split_ref[...], preferred_element_type=F32)
        out_ref[:CAPACITY, :] = both[:, :LANES] + both[:, LANES:]
        meta = lax.dot_general(
            notes, hot, (((1,), (1,)), ((), ())), preferred_element_type=F32
        )
        weight = meta[0:1] + meta[1:2] + meta[2:3]
        where = meta[3:4] * 32.0 + meta[4:5]
        out_ref[CAPACITY:, :] = jnp.concatenate(
            [weight[:, q * LANES : (q + 1) * LANES] for q in range(4)]
            + [where[:, q * LANES : (q + 1) * LANES] for q in range(4)],
            axis=0,
        )


def observe(*refs):
    got_refs, (out_ref, hot_ref, plane_ref) = refs[:OWNERS], refs[OWNERS:]
    total = jnp.zeros((LINES, 2 * LANES), F32)
    weights = jnp.zeros((LINES, 8), F32)
    at = lax.broadcasted_iota(jnp.int32, (LINES, LANES), 0)
    for got_ref in got_refs:
        meta = got_ref[CAPACITY:, :]
        where = meta[4:8].astype(jnp.int32)
        for q in range(4):
            hot = jnp.where(at == where[q : q + 1, :], 1.0, 0.0)
            hot_ref[:, q * LANES : (q + 1) * LANES] = hot.astype(BF16)
        hot = hot_ref[...]
        high, low = halves(got_ref[:CAPACITY, :])
        total += jnp.dot(hot, jnp.concatenate([high, low], axis=1), preferred_element_type=F32)
        weight = jnp.concatenate([meta[q : q + 1] for q in range(4)], axis=1)
        parts = [p.astype(F32) for p in thirds(weight)]
        stacked = jnp.concatenate(parts + [jnp.zeros((5, CAPACITY), F32)], axis=0).astype(BF16)
        weights += lax.dot_general(
            hot, stacked, (((1,), (1,)), ((), ())), preferred_element_type=F32
        )
    weight_sum = weights[:, 0:1] + weights[:, 1:2] + weights[:, 2:3]
    plane_ref[...] = (total[:, :LANES] + total[:, LANES:]) / weight_sum
    store_tiles(plane_ref, out_ref)


def columns_from(got_ref, out_ref):
    for i in range(8):
        turned = got_ref[pl.ds(i, Z, stride=8), :].T
        for j in range(4):
            out_ref[SIDE * (8 * j + i) : SIDE * (8 * j + i) + SIDE, :] = turned[SIDE * j : SIDE * j + SIDE, :]


def store_edges(side_ref, out_ref, own_ref, other_ref, rows=SIDE, rim=RIM):
    skip = (SIDE - rim) * rows
    own_ref[...] = out_ref[pl.ds(pl.multiple_of(side_ref[0] * skip, 8), rim * rows), :]
    other_ref[...] = out_ref[pl.ds(pl.multiple_of((1 - side_ref[0]) * skip, 8), rim * rows), :]


def swap_leading(in_ref, out_ref):
    for i in range(SIDE):
        out_ref[SIDE * i : SIDE * i + SIDE, :] = in_ref[pl.ds(i, SIDE, stride=SIDE), :]


def arrive(side_ref, got_ref, out_ref, swapped_ref, own_ref, other_ref):
    columns_from(got_ref, out_ref)
    swap_leading(out_ref, swapped_ref)
    store_edges(side_ref, swapped_ref, own_ref, other_ref)


def taps_of(taps_ref, flip):
    return [taps_ref[TAPS - 1 - k if flip else k] for k in range(TAPS)]


def correlate(taps, in_ref, cells, leads, rows, shift, store):
    def block(index, carry):
        row = index * 8
        for first in range(0, leads, 8):
            totals = [None] * 8
            for cell in range(max(0, first - shift), min(cells, first + 7 + TAPS - shift)):
                value = in_ref[pl.ds(pl.multiple_of(cell * rows + row, 8), 8), :]
                for i in range(8):
                    k = cell - first - i + shift
                    if 0 <= k < TAPS:
                        term = taps[k] * value
                        totals[i] = term if totals[i] is None else totals[i] + term
            for i in range(8):
                store(first + i, row, jnp.zeros((8, Z), F32) if totals[i] is None else totals[i])
        return carry

    lax.fori_loop(0, rows // 8, block, 0)


def own_share(flip, leads, rows, shift, taps_ref, mid_ref, out_ref):
    def store(lead, row, value):
        out_ref[pl.ds(pl.multiple_of(lead * rows + row, 8), 8), :] = value

    correlate(taps_of(taps_ref, flip), mid_ref, SIDE, leads, rows, shift, store)


def add_rims(taps_ref, flip, side_ref, part_ref, near_ref, far_ref, store, rows=SIDE):
    taps = taps_of(taps_ref, flip)
    side = side_ref[0]
    for row in range(0, rows, 8):
        near = [near_ref[rows * i + row : rows * i + row + 8, :] for i in range(RIM)]
        far = [far_ref[rows * i + row : rows * i + row + 8, :] for i in range(RIM)]
        low = [jnp.where(side == 0, a, b) for a, b in zip(near, far, strict=True)]
        high = [jnp.where(side == 0, b, a) for a, b in zip(near, far, strict=True)]
        for lead in range(SIDE):
            total = part_ref[rows * lead + row : rows * lead + row + 8, :]
            for i in range(RIM):
                if i >= lead:
                    total = total + taps[i - lead] * low[i]
                if i <= lead - SIDE + RIM:
                    total = total + taps[SIDE + RIM + i - lead] * high[i]
            store(lead, row, total)


def swapped(lead, row):
    return pl.ds(SIDE * row + lead, 8, stride=SIDE)


def along_x(taps_ref, side_ref, part_ref, cross_ref, pair_ref, out_ref, own_ref, other_ref):
    def store(lead, row, value):
        out_ref[swapped(lead, row), :] = value

    add_rims(taps_ref, True, side_ref, part_ref, cross_ref, pair_ref, store)
    store_edges(side_ref, out_ref, own_ref, other_ref)


def along_y_first(taps_ref, side_ref, part_ref, near_ref, far_ref, out_ref, cross_ref, pair_ref):
    def store(lead, row, value):
        out_ref[swapped(lead, row), :] = value

    add_rims(taps_ref, False, side_ref, part_ref, near_ref, far_ref, store)
    store_edges(side_ref, out_ref, cross_ref, pair_ref)


def extend(side_ref, tile_ref, near_ref, far_ref, out_ref):
    zeros = jnp.zeros((8, Z), F32)
    for x in range(SIDE):
        out_ref[WIDE * x : WIDE * x + 8, :] = zeros
        out_ref[WIDE * x + WIDE - 8 : WIDE * x + WIDE, :] = zeros
        out_ref[WIDE * x + MARGIN : WIDE * x + MARGIN + SIDE, :] = tile_ref[SIDE * x : SIDE * x + SIDE, :]
    for r in range(RIM):
        for x in range(0, SIDE, 8):
            near = near_ref[SIDE * r + x : SIDE * r + x + 8, :]
            far = far_ref[SIDE * r + x : SIDE * r + x + 8, :]
            below = pl.ds(WIDE * x + r + 1, 8, stride=WIDE)
            above = pl.ds(WIDE * x + MARGIN + SIDE + r, 8, stride=WIDE)
            out_ref[below, :] = jnp.where(side_ref[0] == 0, near, far)
            out_ref[above, :] = jnp.where(side_ref[0] == 0, far, near)


def rim_share(taps, upper, rim_ref, row):
    cells = [rim_ref[SIDE * i + row : SIDE * i + row + 8, :] for i in range(2 * RIM)]
    for n in range(2 * RIM):
        used = range(n + 1) if upper else range(n, 2 * RIM)
        total = None
        for i in used:
            term = taps[2 * RIM + i - n if upper else i - n] * cells[i]
            total = term if total is None else total + term
        yield n, total


def near_share(taps_ref, side_ref, near_ref, out_ref):
    taps = taps_of(taps_ref, True)
    for side in range(2):

        @pl.when(side_ref[0] == side)
        def _():
            for row in range(0, SIDE, 8):
                for n, total in rim_share(taps, side == 1, near_ref, row):
                    out_ref[SIDE * n + row : SIDE * n + row + 8, :] = total


def wide_rows(taps_ref, side_ref, part_ref, near_ref, far_ref, out_ref, cross_ref, pair_ref):
    taps = taps_of(taps_ref, True)
    for side in range(2):

        @pl.when(side_ref[0] == side)
        def _():
            for row in range(0, SIDE, 8):

                def store(e, total):
                    out_ref[pl.ds(WIDE * row + e, 8, stride=WIDE), :] = (
                        part_ref[SIDE * e + row : SIDE * e + row + 8, :] + total
                    )

                for n, total in rim_share(taps, side == 0, far_ref, row):
                    share = near_ref[SIDE * n + row : SIDE * n + row + 8, :]
                    store(1 + n, share if side == 0 else total)
                    store(SIDE + 1 + n, total if side == 0 else share)
                for e in (0, SIDE - 1, SIDE, WIDE - 1):
                    store(e, 0.0)

    store_edges(side_ref, out_ref, cross_ref, pair_ref, WIDE)


def update_wide(
    taps_ref, side_ref, part_ref, cross_ref, pair_ref, start_ref, new_ref, out_ref, own_ref, other_ref, turned_ref
):
    def store(x, e, value):
        spot = slice(WIDE * x + e, WIDE * x + e + 8)
        new = start_ref[spot, :] * value
        new_ref[spot, :] = new
        turned_ref[pl.ds(SIDE * e + x, 8, stride=SIDE), :] = new

    add_rims(taps_ref, True, side_ref, part_ref, cross_ref, pair_ref, store, WIDE)

    def store_y(y, x, value):
        out_ref[swapped(y, x), :] = value

    correlate(taps_of(taps_ref, False), turned_ref, WIDE, SIDE, SIDE, RIM - MARGIN, store_y)
    store_edges(side_ref, out_ref, own_ref, other_ref)


def axial(value, band, back):
    dims = (((1,), (0 if back else 1,)), ((), ()))
    high, low = halves(value)
    band_high, band_low = halves(band)
    double = jnp.concatenate([band_high, band_high], axis=0 if back else 1)
    both = jnp.concatenate([high, low], axis=1)
    return lax.dot_general(both, double, dims, preferred_element_type=F32) + lax.dot_general(
        high, band_low, dims, preferred_element_type=F32
    )


def along_x_last(taps_ref, side_ref, part_ref, cross_ref, pair_ref, cols_ref):
    def store(lead, row, value):
        cols_ref[SIDE * lead + row : SIDE * lead + row + 8, :] = value

    add_rims(taps_ref, False, side_ref, part_ref, cross_ref, pair_ref, store)


def blur(taps_ref, side_ref, part_ref, cross_ref, pair_ref, band_ref, out_ref, cols_ref):
    along_x_last(taps_ref, side_ref, part_ref, cross_ref, pair_ref, cols_ref)
    out_ref[...] = axial(cols_ref[...], band_ref[...], False)


def first_ratio(side_ref, got_ref, blurred_ref, band_ref, seen_ref, out_ref, own_ref, other_ref, cols_ref):
    columns_from(got_ref, seen_ref)
    cols_ref[...] = axial(seen_ref[...] / blurred_ref[...], band_ref[...], True)
    swap_leading(cols_ref, out_ref)
    store_edges(side_ref, out_ref, own_ref, other_ref, rim=2 * RIM)


def blur_ratio(
    taps_ref, side_ref, part_ref, cross_ref, pair_ref, band_ref, seen_ref, out_ref, own_ref, other_ref, cols_ref
):
    along_x_last(taps_ref, side_ref, part_ref, cross_ref, pair_ref, cols_ref)
    band = band_ref[...]
    for start in range(0, SIDE * SIDE, 256):
        spot = slice(start, start + 256)
        ratio = seen_ref[spot, :] / axial(cols_ref[spot, :], band, False)
        out_ref[spot, :] = axial(ratio, band, True)
    store_edges(side_ref, out_ref, own_ref, other_ref)


def last_update(taps_ref, side_ref, part_ref, near_ref, far_ref, estimate_ref, out_ref, cols_ref):
    def store(lead, row, value):
        cols_ref[swapped(lead, row), :] = value

    add_rims(taps_ref, True, side_ref, part_ref, near_ref, far_ref, store)
    for i in range(8):
        block = jnp.concatenate(
            [
                estimate_ref[WIDE * x + MARGIN : WIDE * x + MARGIN + SIDE, :]
                * cols_ref[SIDE * x : SIDE * x + SIDE, :]
                for x in range(i, SIDE, 8)
            ],
            axis=0,
        )
        out_ref[pl.ds(i, Z, stride=8), :] = block.T


FLAT = (SIDE * SIDE, Z)
EDGE = (RIM * SIDE, Z)
WIDE_FLAT = (SIDE * WIDE, Z)
WIDE_EDGE = (RIM * WIDE, Z)
WIDE_RIM = (2 * RIM * SIDE, Z)
PIECES = (Z, 8, LANES)


def shards(camera_rows, blend, route, line, start, psf_xy, psf_z):
    slabs, reps = lax.axis_size("slab"), lax.axis_size("rep")
    x_tiles = LINES // SIDE
    y_tiles = slabs // x_tiles
    chunks = camera_rows.shape[0] // LANES
    pair_swaps = [(t, t ^ 1) for t in range(slabs)]
    cross_swaps = []
    for t in range(1, slabs, 2):
        if t % x_tiles != x_tiles - 1:
            cross_swaps += [(t, t + 1), (t + 1, t)]
    side = (lax.axis_index("slab") % 2).reshape(1)
    y_pairs = []
    for t in range(slabs):
        for r in range(reps):
            y = r * y_tiles + t // x_tiles + 1
            if y < y_tiles * reps:
                up = (y % y_tiles) * x_tiles + t % x_tiles
                y_pairs.append((t * reps + r, up * reps + y // y_tiles))

    def rims_x(cross, pair):
        return lax.ppermute(cross, "slab", cross_swaps), lax.ppermute(pair, "slab", pair_swaps)

    y_one, y_two = [], []
    for low, high in y_pairs:
        upward, downward = (y_one, y_two) if (low // reps) % 2 == 0 else (y_two, y_one)
        upward.append((low, high))
        downward.append((high, low))

    def rims_y(own, other):
        axes = ("slab", "rep")
        return lax.ppermute(other, axes, y_one), lax.ppermute(own, axes, y_two)

    def turn(pieces):
        return lax.all_to_all(pieces, "slab", split_axis=0, concat_axis=0, tiled=True)

    taps = psf_xy / jnp.sum(psf_xy)

    arrived = turn(call(store_tiles, [PIECES], [], start.reshape(LINES, LANES))[0])
    band = call(axial_band, [(Z, LANES)], [((8, LANES), F32)], psf_z[None, :])[0]
    sent = call(
        pack_rows,
        [(CAPACITY + META, LANES)] * OWNERS,
        [((chunks * LANES, 2 * LANES), BF16), ((CAPACITY, chunks * LANES), BF16)],
        lax.axis_index("rep").reshape(1),
        camera_rows,
        blend.reshape(chunks, LANES),
        route.reshape(chunks, LANES),
        line.reshape(chunks, LANES),
        smem=1,
    )
    got = [
        block if step == 0 else lax.ppermute(block, "rep", [(r, (r + step) % reps) for r in range(reps)])
        for step, block in enumerate(sent)
    ]
    seen_pieces = call(observe, [PIECES], [((LINES, CAPACITY), BF16), ((LINES, LANES), F32)], *got)[0]
    arrived, seen_pieces = lax.optimization_barrier((arrived, seen_pieces))
    estimate, flipped, *edges = call(
        arrive, [FLAT, FLAT, EDGE, EDGE], [], side, arrived.reshape(Z * 8, LANES), smem=1
    )
    seen_arrived = turn(seen_pieces)

    def own(flip, value, rows=SIDE):
        kernel = functools.partial(own_share, flip, SIDE, rows, RIM)
        return call(kernel, [(SIDE * rows, Z)], [], taps, value, smem=1)[0]

    cols = [(FLAT, F32)]
    start_rims = rims_y(*edges)
    value, *edges = call(
        along_y_first, [FLAT, EDGE, EDGE], [], taps, side, own(False, flipped), *start_rims, smem=2
    )
    blurred = call(blur, [FLAT], cols, taps, side, own(False, value), *rims_x(*edges), band, smem=2)[0]
    seen, back, *edges = call(
        first_ratio,
        [FLAT, FLAT, WIDE_RIM, WIDE_RIM],
        cols,
        side,
        seen_arrived.reshape(Z * 8, LANES),
        blurred,
        band,
        smem=1,
    )
    near, far = rims_y(*edges)
    part = call(
        functools.partial(own_share, True, WIDE, SIDE, RIM + MARGIN), [WIDE_FLAT], [], taps, back, smem=1
    )[0]
    near = call(near_share, [WIDE_RIM], [], taps, side, near, smem=2)[0]
    value, *edges = call(
        wide_rows, [WIDE_FLAT, WIDE_EDGE, WIDE_EDGE], [], taps, side, part, near, far, smem=2
    )
    rims = rims_x(*edges)
    wide = call(extend, [WIDE_FLAT], [], side, estimate, *start_rims, smem=1)[0]
    wide, value, *edges = call(
        update_wide,
        [WIDE_FLAT, FLAT, EDGE, EDGE],
        [(WIDE_FLAT, F32)],
        taps,
        side,
        own(True, value, WIDE),
        *rims,
        wide,
        smem=2,
    )
    rims = rims_x(*edges)
    back, *edges = call(
        blur_ratio, [FLAT, EDGE, EDGE], cols, taps, side, own(False, value), *rims, band, seen, smem=2
    )
    rims = rims_x(*edges)
    value, *edges = call(along_x, [FLAT, EDGE, EDGE], [], taps, side, own(True, back), *rims, smem=2)
    rims = rims_y(*edges)
    pieces = call(
        last_update, [(Z * 8, LANES)], cols, taps, side, own(True, value), *rims, wide, smem=2
    )[0]
    done = turn(pieces.reshape(PIECES))
    plane = call(plane_of, [(LINES, LANES)], [], done)[0]
    return plane.reshape(1, LINES, LANES)


def solution(mesh):
    in_specs = (
        P(("slab", "rep"), None),
        P(("slab", "rep")),
        P(("slab", "rep")),
        P(("slab", "rep")),
        P("slab", None, "rep"),
        P(),
        P(),
    )
    out_specs = P("slab", None, "rep")
    return jax.shard_map(shards, mesh=mesh, in_specs=in_specs, out_specs=out_specs, check_vma=False)
```

```python
import functools

import jax
import jax.numpy as jnp
from jax import lax
from jax.experimental import pallas as pl
from jax.experimental.pallas import tpu as pltpu
from jax.sharding import PartitionSpec as P

F32 = jnp.float32
BF16 = jnp.bfloat16
LANES = 128
SIDE = 32
TAPS = 31
RIM = TAPS // 2
WIDE = 64
MARGIN = 16
OWNERS = 4
CAPACITY = 512
META = 8
LINES = 1024
Z = 128
VMEM_LIMIT = 40 * 1024 * 1024


def call(kernel, out_shapes, scratch, *args, smem=0):
    specs = [
        pl.BlockSpec(memory_space=pltpu.SMEM if i < smem else pltpu.VMEM)
        for i in range(len(args))
    ]
    outs = tuple(jax.ShapeDtypeStruct(s, F32) for s in out_shapes)
    return pl.pallas_call(
        kernel,
        out_shape=outs,
        in_specs=specs,
        out_specs=tuple(pl.BlockSpec(memory_space=pltpu.VMEM) for _ in outs),
        scratch_shapes=[pltpu.VMEM(s, d) for s, d in scratch],
        compiler_params=pltpu.CompilerParams(vmem_limit_bytes=VMEM_LIMIT),
        name=kernel.func.__name__ if isinstance(kernel, functools.partial) else kernel.__name__,
    )(*args)


def halves(value):
    high = value.astype(BF16)
    return high, (value - high.astype(F32)).astype(BF16)


def thirds(value):
    high, rest = halves(value)
    low = (value - high.astype(F32) - rest.astype(F32)).astype(BF16)
    return high, rest, low


def swap_lanes(pairs, first, moves):
    mixed = [jnp.where(first, b, a) for a, b in pairs]
    up = [pltpu.roll(m, moves[0], axis=1) for m in mixed]
    down = up if moves[0] == moves[1] else [pltpu.roll(m, moves[1], axis=1) for m in mixed]
    return [
        (jnp.where(first, a, u), jnp.where(first, d, b)) for (a, b), u, d in zip(pairs, up, down, strict=True)
    ]


def lane_blocks(pieces):
    lane = lax.broadcasted_iota(jnp.int32, (8, LANES), 1)
    outer = swap_lanes([pair for a, b, c, d in pieces for pair in ((a, c), (b, d))], lane < 64, (64, 64))
    rows = [(ac[0], bd[0], ac[1], bd[1]) for ac, bd in zip(outer[::2], outer[1::2], strict=True)]
    inner = swap_lanes([pair for a, b, c, d in rows for pair in ((a, b), (c, d))], lane % 64 < 32, (32, 96))
    return [ab + cd for ab, cd in zip(inner[::2], inner[1::2], strict=True)]


def store_tiles(plane_ref, out_ref):
    for first in range(0, 32, 8):
        parts = range(first, first + 8)
        rows = [
            tuple(plane_ref[SIDE * p + 8 * j : SIDE * p + 8 * j + 8, :] for j in range(4)) for p in parts
        ]
        for part, piece in zip(parts, lane_blocks(rows), strict=True):
            for sub in range(4):
                out_ref[32 * sub + part] = piece[sub]


def plane_of(got_ref, out_ref):
    for first in range(0, 32, 8):
        parts = range(first, first + 8)
        pieces = [tuple(got_ref[32 * sub + p] for sub in range(4)) for p in parts]
        for part, rows in zip(parts, lane_blocks(pieces), strict=True):
            for j in range(4):
                out_ref[SIDE * part + 8 * j : SIDE * part + 8 * j + 8, :] = rows[j]


def axial_band(psf_ref, out_ref, row_ref):
    row_ref[...] = jnp.zeros((8, LANES), F32)
    row_ref[0:1, : psf_ref.shape[1]] = psf_ref[...]
    psf = row_ref[0:1, :]
    rows = jnp.broadcast_to(psf / jnp.sum(psf, axis=1, keepdims=True), (Z, LANES))
    rolled = pltpu.roll(rows, LANES - 31, axis=1, stride=1, stride_axis=0)
    a = lax.broadcasted_iota(jnp.int32, (Z, LANES), 0)
    b = lax.broadcasted_iota(jnp.int32, (Z, LANES), 1)
    out_ref[...] = jnp.where(jnp.abs(a - b) <= 31, rolled, 0.0)


def pack_rows(rep_ref, rows_ref, blend_ref, route_ref, line_ref, *refs):
    out_refs, (split_ref, hot_ref) = refs[:OWNERS], refs[OWNERS:]
    chunks = rows_ref.shape[0] // LANES
    blend = blend_ref[...]
    route = route_ref[...]
    line = line_ref[...]
    i = lax.broadcasted_iota(jnp.int32, (LANES, LANES), 0)
    j = lax.broadcasted_iota(jnp.int32, (LANES, LANES), 1)
    upto = (i <= j).astype(BF16)
    ones = jnp.ones((LANES, LANES), BF16)
    ci = lax.broadcasted_iota(jnp.int32, (16, 16), 0)
    cj = lax.broadcasted_iota(jnp.int32, (16, 16), 1)
    before = (cj < ci).astype(BF16)
    key = route * CAPACITY
    for owner in range(OWNERS):
        mine = (route == owner).astype(F32)
        mine16 = jnp.concatenate([mine, jnp.zeros((16 - chunks, LANES), F32)], axis=0).astype(BF16)
        upto_here = jnp.dot(mine16, upto, preferred_element_type=F32)
        totals = jnp.dot(mine16, ones, preferred_element_type=F32).astype(BF16)
        offset = jnp.dot(before, totals, preferred_element_type=F32)
        rank = (upto_here + offset)[:chunks] - 1.0
        key = key + jnp.where(route == owner, rank, 0.0).astype(jnp.int32)
    square = jnp.concatenate([blend, jnp.zeros((LANES - chunks, LANES), F32)], axis=0)
    columns = square.T
    for c in range(chunks):
        weighted = rows_ref[c * LANES : (c + 1) * LANES, :] * columns[:, c : c + 1]
        high, low = halves(weighted)
        split_ref[c * LANES : (c + 1) * LANES, :LANES] = high
        split_ref[c * LANES : (c + 1) * LANES, LANES:] = low
    first, second, third = thirds(blend)
    upper = line // 32
    parts = [first, second, third, upper.astype(BF16), (line - upper * 32).astype(BF16)]
    notes = jnp.concatenate(
        [
            jnp.concatenate(
                [p.astype(F32)[c : c + 1] for p in parts] + [jnp.zeros((3, LANES), F32)], axis=0
            )
            for c in range(chunks)
        ],
        axis=1,
    ).astype(BF16)
    for step, out_ref in enumerate(out_refs):
        owner = (rep_ref[0] + step) % OWNERS
        slot = lax.broadcasted_iota(jnp.int32, (CAPACITY, LANES), 0) + owner * CAPACITY
        for c in range(chunks):
            hot = jnp.where(slot == key[c : c + 1, :], 1.0, 0.0)
            hot_ref[:, c * LANES : (c + 1) * LANES] = hot.astype(BF16)
        hot = hot_ref[...]
        both = jnp.dot(hot, split_ref[...], preferred_element_type=F32)
        out_ref[:CAPACITY, :] = both[:, :LANES] + both[:, LANES:]
        meta = lax.dot_general(
            notes, hot, (((1,), (1,)), ((), ())), preferred_element_type=F32
        )
        weight = meta[0:1] + meta[1:2] + meta[2:3]
        where = meta[3:4] * 32.0 + meta[4:5]
        out_ref[CAPACITY:, :] = jnp.concatenate(
            [weight[:, q * LANES : (q + 1) * LANES] for q in range(4)]
            + [where[:, q * LANES : (q + 1) * LANES] for q in range(4)],
            axis=0,
        )


def observe(*refs):
    got_refs, (out_ref, hot_ref, plane_ref) = refs[:OWNERS], refs[OWNERS:]
    total = jnp.zeros((LINES, 2 * LANES), F32)
    weights = jnp.zeros((LINES, 8), F32)
    at = lax.broadcasted_iota(jnp.int32, (LINES, LANES), 0)
    for got_ref in got_refs:
        meta = got_ref[CAPACITY:, :]
        where = meta[4:8].astype(jnp.int32)
        for q in range(4):
            hot = jnp.where(at == where[q : q + 1, :], 1.0, 0.0)
            hot_ref[:, q * LANES : (q + 1) * LANES] = hot.astype(BF16)
        hot = hot_ref[...]
        high, low = halves(got_ref[:CAPACITY, :])
        total += jnp.dot(hot, jnp.concatenate([high, low], axis=1), preferred_element_type=F32)
        weight = jnp.concatenate([meta[q : q + 1] for q in range(4)], axis=1)
        parts = [p.astype(F32) for p in thirds(weight)]
        stacked = jnp.concatenate(parts + [jnp.zeros((5, CAPACITY), F32)], axis=0).astype(BF16)
        weights += lax.dot_general(
            hot, stacked, (((1,), (1,)), ((), ())), preferred_element_type=F32
        )
    weight_sum = weights[:, 0:1] + weights[:, 1:2] + weights[:, 2:3]
    plane_ref[...] = (total[:, :LANES] + total[:, LANES:]) / weight_sum
    store_tiles(plane_ref, out_ref)


def columns_from(got_ref, out_ref):
    for i in range(8):
        turned = got_ref[pl.ds(i, Z, stride=8), :].T
        for j in range(4):
            out_ref[SIDE * (8 * j + i) : SIDE * (8 * j + i) + SIDE, :] = turned[SIDE * j : SIDE * j + SIDE, :]


def store_edges(side_ref, out_ref, own_ref, other_ref, rows=SIDE, rim=RIM):
    skip = (SIDE - rim) * rows
    own_ref[...] = out_ref[pl.ds(pl.multiple_of(side_ref[0] * skip, 8), rim * rows), :]
    other_ref[...] = out_ref[pl.ds(pl.multiple_of((1 - side_ref[0]) * skip, 8), rim * rows), :]


def swap_leading(in_ref, out_ref):
    for i in range(SIDE):
        out_ref[SIDE * i : SIDE * i + SIDE, :] = in_ref[pl.ds(i, SIDE, stride=SIDE), :]


def arrive(side_ref, got_ref, out_ref, swapped_ref, own_ref, other_ref):
    columns_from(got_ref, out_ref)
    swap_leading(out_ref, swapped_ref)
    store_edges(side_ref, swapped_ref, own_ref, other_ref)


def taps_of(taps_ref, flip):
    return [taps_ref[TAPS - 1 - k if flip else k] for k in range(TAPS)]


def correlate(taps, in_ref, cells, leads, rows, shift, store):
    def block(index, carry):
        row = index * 8
        for first in range(0, leads, 8):
            totals = [None] * 8
            for cell in range(max(0, first - shift), min(cells, first + 7 + TAPS - shift)):
                value = in_ref[pl.ds(pl.multiple_of(cell * rows + row, 8), 8), :]
                for i in range(8):
                    k = cell - first - i + shift
                    if 0 <= k < TAPS:
                        term = taps[k] * value
                        totals[i] = term if totals[i] is None else totals[i] + term
            for i in range(8):
                store(first + i, row, jnp.zeros((8, Z), F32) if totals[i] is None else totals[i])
        return carry

    lax.fori_loop(0, rows // 8, block, 0)


def own_share(flip, leads, rows, shift, taps_ref, mid_ref, out_ref):
    def store(lead, row, value):
        out_ref[pl.ds(pl.multiple_of(lead * rows + row, 8), 8), :] = value

    correlate(taps_of(taps_ref, flip), mid_ref, SIDE, leads, rows, shift, store)


def add_rims(taps_ref, flip, side_ref, part_ref, near_ref, far_ref, store, rows=SIDE):
    taps = taps_of(taps_ref, flip)
    side = side_ref[0]
    for row in range(0, rows, 8):
        near = [near_ref[rows * i + row : rows * i + row + 8, :] for i in range(RIM)]
        far = [far_ref[rows * i + row : rows * i + row + 8, :] for i in range(RIM)]
        low = [jnp.where(side == 0, a, b) for a, b in zip(near, far, strict=True)]
        high = [jnp.where(side == 0, b, a) for a, b in zip(near, far, strict=True)]
        for lead in range(SIDE):
            total = part_ref[rows * lead + row : rows * lead + row + 8, :]
            for i in range(RIM):
                if i >= lead:
                    total = total + taps[i - lead] * low[i]
                if i <= lead - SIDE + RIM:
                    total = total + taps[SIDE + RIM + i - lead] * high[i]
            store(lead, row, total)


def swapped(lead, row):
    return pl.ds(SIDE * row + lead, 8, stride=SIDE)


def along_y_first(taps_ref, side_ref, part_ref, near_ref, far_ref, out_ref, cross_ref, pair_ref):
    def store(lead, row, value):
        out_ref[swapped(lead, row), :] = value

    add_rims(taps_ref, False, side_ref, part_ref, near_ref, far_ref, store)
    store_edges(side_ref, out_ref, cross_ref, pair_ref)


def extend(side_ref, tile_ref, near_ref, far_ref, out_ref):
    zeros = jnp.zeros((8, Z), F32)
    for x in range(SIDE):
        out_ref[WIDE * x : WIDE * x + 8, :] = zeros
        out_ref[WIDE * x + WIDE - 8 : WIDE * x + WIDE, :] = zeros
        out_ref[WIDE * x + MARGIN : WIDE * x + MARGIN + SIDE, :] = tile_ref[SIDE * x : SIDE * x + SIDE, :]
    for r in range(RIM):
        for x in range(0, SIDE, 8):
            near = near_ref[SIDE * r + x : SIDE * r + x + 8, :]
            far = far_ref[SIDE * r + x : SIDE * r + x + 8, :]
            below = pl.ds(WIDE * x + r + 1, 8, stride=WIDE)
            above = pl.ds(WIDE * x + MARGIN + SIDE + r, 8, stride=WIDE)
            out_ref[below, :] = jnp.where(side_ref[0] == 0, near, far)
            out_ref[above, :] = jnp.where(side_ref[0] == 0, far, near)


def rim_share(taps, upper, rim_ref, row):
    cells = [rim_ref[SIDE * i + row : SIDE * i + row + 8, :] for i in range(2 * RIM)]
    for n in range(2 * RIM):
        used = range(n + 1) if upper else range(n, 2 * RIM)
        total = None
        for i in used:
            term = taps[2 * RIM + i - n if upper else i - n] * cells[i]
            total = term if total is None else total + term
        yield n, total


def near_share(taps_ref, side_ref, rim_ref, out_ref):
    taps = taps_of(taps_ref, True)
    for side in range(2):

        @pl.when(side_ref[0] == side)
        def _():
            for row in range(0, SIDE, 8):
                for n, total in rim_share(taps, side == 1, rim_ref, row):
                    out_ref[SIDE * n + row : SIDE * n + row + 8, :] = total


def wide_rows(taps_ref, side_ref, part_ref, near_ref, far_ref, out_ref, cross_ref, pair_ref):
    taps = taps_of(taps_ref, True)
    for side in range(2):

        @pl.when(side_ref[0] == side)
        def _():
            for row in range(0, SIDE, 8):

                def store(e, total):
                    out_ref[pl.ds(WIDE * row + e, 8, stride=WIDE), :] = (
                        part_ref[SIDE * e + row : SIDE * e + row + 8, :] + total
                    )

                for n, total in rim_share(taps, side == 0, far_ref, row):
                    share = near_ref[SIDE * n + row : SIDE * n + row + 8, :]
                    store(1 + n, share if side == 0 else total)
                    store(SIDE + 1 + n, total if side == 0 else share)
                for e in (0, SIDE - 1, SIDE, WIDE - 1):
                    store(e, 0.0)

    store_edges(side_ref, out_ref, cross_ref, pair_ref, WIDE)


def update_wide(
    taps_ref,
    side_ref,
    part_ref,
    cross_ref,
    pair_ref,
    start_ref,
    new_ref,
    out_ref,
    cross_out_ref,
    pair_out_ref,
    turned_ref,
):
    def store(x, e, value):
        spot = slice(WIDE * x + e, WIDE * x + e + 8)
        new = start_ref[spot, :] * value
        new_ref[spot, :] = new
        turned_ref[pl.ds(SIDE * e + x, 8, stride=SIDE), :] = new

    add_rims(taps_ref, True, side_ref, part_ref, cross_ref, pair_ref, store, WIDE)

    def store_y(y, x, value):
        out_ref[swapped(y, x), :] = value

    correlate(taps_of(taps_ref, False), turned_ref, WIDE, SIDE, SIDE, RIM - MARGIN, store_y)
    store_edges(side_ref, out_ref, cross_out_ref, pair_out_ref, rim=2 * RIM)


def axial(value, band, back):
    dims = (((1,), (0 if back else 1,)), ((), ()))
    high, low = halves(value)
    band_high, band_low = halves(band)
    double = jnp.concatenate([band_high, band_high], axis=0 if back else 1)
    both = jnp.concatenate([high, low], axis=1)
    return lax.dot_general(both, double, dims, preferred_element_type=F32) + lax.dot_general(
        high, band_low, dims, preferred_element_type=F32
    )


def along_x_last(taps_ref, side_ref, part_ref, cross_ref, pair_ref, cols_ref):
    def store(lead, row, value):
        cols_ref[SIDE * lead + row : SIDE * lead + row + 8, :] = value

    add_rims(taps_ref, False, side_ref, part_ref, cross_ref, pair_ref, store)


def blur(taps_ref, side_ref, part_ref, cross_ref, pair_ref, band_ref, out_ref, cols_ref):
    along_x_last(taps_ref, side_ref, part_ref, cross_ref, pair_ref, cols_ref)
    out_ref[...] = axial(cols_ref[...], band_ref[...], False)


def first_ratio(
    side_ref,
    got_ref,
    blurred_ref,
    band_ref,
    seen_ref,
    cross_ref,
    pair_ref,
    out_ref,
    own_ref,
    other_ref,
    cols_ref,
):
    columns_from(got_ref, seen_ref)
    cols_ref[...] = axial(seen_ref[...] / blurred_ref[...], band_ref[...], True)
    swap_leading(cols_ref, out_ref)
    store_edges(side_ref, out_ref, own_ref, other_ref, rim=2 * RIM)
    store_edges(side_ref, seen_ref, cross_ref, pair_ref)


def extend_x(side_ref, tile_ref, cross_ref, pair_ref, out_ref):
    ones = jnp.ones((SIDE, Z), F32)
    out_ref[:SIDE, :] = ones
    out_ref[SIDE * (WIDE - 1) :, :] = ones
    out_ref[SIDE * MARGIN : SIDE * (MARGIN + SIDE), :] = tile_ref[...]
    low_at, high_at = SIDE, SIDE * (MARGIN + SIDE)
    cross_at = pl.multiple_of(jnp.where(side_ref[0] == 0, low_at, high_at), 8)
    pair_at = pl.multiple_of(jnp.where(side_ref[0] == 0, high_at, low_at), 8)
    out_ref[pl.ds(cross_at, RIM * SIDE), :] = cross_ref[...]
    out_ref[pl.ds(pair_at, RIM * SIDE), :] = pair_ref[...]


def blur_ratio(
    taps_ref,
    side_ref,
    part_ref,
    cross_ref,
    pair_ref,
    band_ref,
    seen_ref,
    out_ref,
    own_ref,
    other_ref,
    cols_ref,
    ratio_ref,
):
    taps = taps_of(taps_ref, False)
    for side in range(2):

        @pl.when(side_ref[0] == side)
        def _():
            for row in range(0, SIDE, 8):

                def store(e, total):
                    spot = slice(SIDE * e + row, SIDE * e + row + 8)
                    cols_ref[spot, :] = part_ref[spot, :] + total

                low_ref, high_ref = (cross_ref, pair_ref) if side == 0 else (pair_ref, cross_ref)
                for n, total in rim_share(taps, False, low_ref, row):
                    store(1 + n, total)
                for n, total in rim_share(taps, True, high_ref, row):
                    store(SIDE + 1 + n, total)
                for e in (0, SIDE - 1, SIDE, WIDE - 1):
                    store(e, 1.0 if e in (0, WIDE - 1) else 0.0)

    band = band_ref[...]
    for start in range(0, WIDE * SIDE, 256):
        spot = slice(start, start + 256)
        ratio = seen_ref[spot, :] / axial(cols_ref[spot, :], band, False)
        ratio_ref[spot, :] = axial(ratio, band, True)

    def store_x(x, y, value):
        out_ref[swapped(x, y), :] = value

    correlate(taps_of(taps_ref, True), ratio_ref, WIDE, SIDE, SIDE, RIM - MARGIN, store_x)
    store_edges(side_ref, out_ref, own_ref, other_ref)


def last_update(taps_ref, side_ref, part_ref, near_ref, far_ref, estimate_ref, out_ref, cols_ref):
    def store(lead, row, value):
        cols_ref[swapped(lead, row), :] = value

    add_rims(taps_ref, True, side_ref, part_ref, near_ref, far_ref, store)
    for i in range(8):
        block = jnp.concatenate(
            [
                estimate_ref[WIDE * x + MARGIN : WIDE * x + MARGIN + SIDE, :]
                * cols_ref[SIDE * x : SIDE * x + SIDE, :]
                for x in range(i, SIDE, 8)
            ],
            axis=0,
        )
        out_ref[pl.ds(i, Z, stride=8), :] = block.T


FLAT = (SIDE * SIDE, Z)
EDGE = (RIM * SIDE, Z)
WIDE_FLAT = (SIDE * WIDE, Z)
WIDE_EDGE = (RIM * WIDE, Z)
WIDE_RIM = (2 * RIM * SIDE, Z)
PIECES = (Z, 8, LANES)


def shards(camera_rows, blend, route, line, start, psf_xy, psf_z):
    slabs, reps = lax.axis_size("slab"), lax.axis_size("rep")
    x_tiles = LINES // SIDE
    y_tiles = slabs // x_tiles
    chunks = camera_rows.shape[0] // LANES
    pair_swaps = [(t, t ^ 1) for t in range(slabs)]
    cross_swaps = []
    for t in range(1, slabs, 2):
        if t % x_tiles != x_tiles - 1:
            cross_swaps += [(t, t + 1), (t + 1, t)]
    side = (lax.axis_index("slab") % 2).reshape(1)
    y_pairs = []
    for t in range(slabs):
        for r in range(reps):
            y = r * y_tiles + t // x_tiles + 1
            if y < y_tiles * reps:
                up = (y % y_tiles) * x_tiles + t % x_tiles
                y_pairs.append((t * reps + r, up * reps + y // y_tiles))

    def rims_x(cross, pair):
        return lax.ppermute(cross, "slab", cross_swaps), lax.ppermute(pair, "slab", pair_swaps)

    y_one, y_two = [], []
    for low, high in y_pairs:
        upward, downward = (y_one, y_two) if (low // reps) % 2 == 0 else (y_two, y_one)
        upward.append((low, high))
        downward.append((high, low))

    def rims_y(own, other):
        axes = ("slab", "rep")
        return lax.ppermute(other, axes, y_one), lax.ppermute(own, axes, y_two)

    def turn(pieces):
        return lax.all_to_all(pieces, "slab", split_axis=0, concat_axis=0, tiled=True)

    taps = psf_xy / jnp.sum(psf_xy)

    arrived = turn(call(store_tiles, [PIECES], [], start.reshape(LINES, LANES))[0])
    band = call(axial_band, [(Z, LANES)], [((8, LANES), F32)], psf_z[None, :])[0]
    sent = call(
        pack_rows,
        [(CAPACITY + META, LANES)] * OWNERS,
        [((chunks * LANES, 2 * LANES), BF16), ((CAPACITY, chunks * LANES), BF16)],
        lax.axis_index("rep").reshape(1),
        camera_rows,
        blend.reshape(chunks, LANES),
        route.reshape(chunks, LANES),
        line.reshape(chunks, LANES),
        smem=1,
    )
    got = [
        block if step == 0 else lax.ppermute(block, "rep", [(r, (r + step) % reps) for r in range(reps)])
        for step, block in enumerate(sent)
    ]
    seen_pieces = call(observe, [PIECES], [((LINES, CAPACITY), BF16), ((LINES, LANES), F32)], *got)[0]
    arrived, seen_pieces = lax.optimization_barrier((arrived, seen_pieces))
    estimate, flipped, *edges = call(
        arrive, [FLAT, FLAT, EDGE, EDGE], [], side, arrived.reshape(Z * 8, LANES), smem=1
    )
    seen_arrived = turn(seen_pieces)

    def own(flip, value, rows=SIDE):
        kernel = functools.partial(own_share, flip, SIDE, rows, RIM)
        return call(kernel, [(SIDE * rows, Z)], [], taps, value, smem=1)[0]

    cols = [(FLAT, F32)]
    start_rims = rims_y(*edges)
    value, *edges = call(
        along_y_first, [FLAT, EDGE, EDGE], [], taps, side, own(False, flipped), *start_rims, smem=2
    )
    blurred = call(blur, [FLAT], cols, taps, side, own(False, value), *rims_x(*edges), band, smem=2)[0]
    seen, seen_cross, seen_pair, back, *edges = call(
        first_ratio,
        [FLAT, EDGE, EDGE, FLAT, WIDE_RIM, WIDE_RIM],
        cols,
        side,
        seen_arrived.reshape(Z * 8, LANES),
        blurred,
        band,
        smem=1,
    )

    def wide_own(flip, value):
        kernel = functools.partial(own_share, flip, WIDE, SIDE, RIM + MARGIN)
        return call(kernel, [WIDE_FLAT], [], taps, value, smem=1)[0]

    near, far = rims_y(*edges)
    part = wide_own(True, back)
    seen_cross, seen_pair, part = lax.optimization_barrier((seen_cross, seen_pair, part))
    near, *seen_rims = lax.optimization_barrier((near, *rims_x(seen_cross, seen_pair)))
    near = call(near_share, [WIDE_RIM], [], taps, side, near, smem=2)[0]
    value, *edges = call(
        wide_rows, [WIDE_FLAT, WIDE_EDGE, WIDE_EDGE], [], taps, side, part, near, far, smem=2
    )
    rims = rims_x(*edges)
    wide = call(extend, [WIDE_FLAT], [], side, estimate, *start_rims, smem=1)[0]
    wide, value, *edges = call(
        update_wide,
        [WIDE_FLAT, FLAT, WIDE_RIM, WIDE_RIM],
        [(WIDE_FLAT, F32)],
        taps,
        side,
        own(True, value, WIDE),
        *rims,
        wide,
        smem=2,
    )
    rims = rims_x(*edges)
    seen = call(extend_x, [WIDE_FLAT], [], side, seen, *seen_rims, smem=1)[0]
    value, *edges = call(
        blur_ratio,
        [FLAT, EDGE, EDGE],
        [(WIDE_FLAT, F32), (WIDE_FLAT, F32)],
        taps,
        side,
        wide_own(False, value),
        *rims,
        band,
        seen,
        smem=2,
    )
    rims = rims_y(*edges)
    pieces = call(
        last_update, [(Z * 8, LANES)], cols, taps, side, own(True, value), *rims, wide, smem=2
    )[0]
    done = turn(pieces.reshape(PIECES))
    plane = call(plane_of, [(LINES, LANES)], [], done)[0]
    return plane.reshape(1, LINES, LANES)


def solution(mesh):
    in_specs = (
        P(("slab", "rep"), None),
        P(("slab", "rep")),
        P(("slab", "rep")),
        P(("slab", "rep")),
        P("slab", None, "rep"),
        P(),
        P(),
    )
    out_specs = P("slab", None, "rep")
    return jax.shard_map(shards, mesh=mesh, in_specs=in_specs, out_specs=out_specs, check_vma=False)
```

```python
import functools

import jax
import jax.numpy as jnp
from jax import lax
from jax.experimental import pallas as pl
from jax.experimental.pallas import tpu as pltpu
from jax.sharding import PartitionSpec as P

F32 = jnp.float32
BF16 = jnp.bfloat16
LANES = 128
SIDE = 32
TAPS = 31
RIM = TAPS // 2
WIDE = 64
MARGIN = 16
OWNERS = 4
CAPACITY = 512
META = 8
LINES = 1024
Z = 128
VMEM_LIMIT = 40 * 1024 * 1024


def call(kernel, out_shapes, scratch, *args, smem=0):
    specs = [
        pl.BlockSpec(memory_space=pltpu.SMEM if i < smem else pltpu.VMEM)
        for i in range(len(args))
    ]
    outs = tuple(jax.ShapeDtypeStruct(s, F32) for s in out_shapes)
    return pl.pallas_call(
        kernel,
        out_shape=outs,
        in_specs=specs,
        out_specs=tuple(pl.BlockSpec(memory_space=pltpu.VMEM) for _ in outs),
        scratch_shapes=[pltpu.VMEM(s, d) for s, d in scratch],
        compiler_params=pltpu.CompilerParams(vmem_limit_bytes=VMEM_LIMIT),
        name=kernel.func.__name__ if isinstance(kernel, functools.partial) else kernel.__name__,
    )(*args)


def halves(value):
    high = value.astype(BF16)
    return high, (value - high.astype(F32)).astype(BF16)


def thirds(value):
    high, rest = halves(value)
    low = (value - high.astype(F32) - rest.astype(F32)).astype(BF16)
    return high, rest, low


def swap_lanes(pairs, first, moves):
    mixed = [jnp.where(first, b, a) for a, b in pairs]
    up = [pltpu.roll(m, moves[0], axis=1) for m in mixed]
    down = up if moves[0] == moves[1] else [pltpu.roll(m, moves[1], axis=1) for m in mixed]
    return [
        (jnp.where(first, a, u), jnp.where(first, d, b)) for (a, b), u, d in zip(pairs, up, down, strict=True)
    ]


def lane_blocks(pieces):
    lane = lax.broadcasted_iota(jnp.int32, (8, LANES), 1)
    outer = swap_lanes([pair for a, b, c, d in pieces for pair in ((a, c), (b, d))], lane < 64, (64, 64))
    rows = [(ac[0], bd[0], ac[1], bd[1]) for ac, bd in zip(outer[::2], outer[1::2], strict=True)]
    inner = swap_lanes([pair for a, b, c, d in rows for pair in ((a, b), (c, d))], lane % 64 < 32, (32, 96))
    return [ab + cd for ab, cd in zip(inner[::2], inner[1::2], strict=True)]


def store_tiles(plane_ref, out_ref):
    for first in range(0, 32, 8):
        parts = range(first, first + 8)
        rows = [
            tuple(plane_ref[SIDE * p + 8 * j : SIDE * p + 8 * j + 8, :] for j in range(4)) for p in parts
        ]
        for part, piece in zip(parts, lane_blocks(rows), strict=True):
            for sub in range(4):
                out_ref[32 * sub + part] = piece[sub]


def plane_of(got_ref, out_ref):
    for first in range(0, 32, 8):
        parts = range(first, first + 8)
        pieces = [tuple(got_ref[32 * sub + p] for sub in range(4)) for p in parts]
        for part, rows in zip(parts, lane_blocks(pieces), strict=True):
            for j in range(4):
                out_ref[SIDE * part + 8 * j : SIDE * part + 8 * j + 8, :] = rows[j]


def axial_band(psf_ref, out_ref, row_ref):
    row_ref[...] = jnp.zeros((8, LANES), F32)
    row_ref[0:1, : psf_ref.shape[1]] = psf_ref[...]
    psf = row_ref[0:1, :]
    rows = jnp.broadcast_to(psf / jnp.sum(psf, axis=1, keepdims=True), (Z, LANES))
    rolled = pltpu.roll(rows, LANES - 31, axis=1, stride=1, stride_axis=0)
    a = lax.broadcasted_iota(jnp.int32, (Z, LANES), 0)
    b = lax.broadcasted_iota(jnp.int32, (Z, LANES), 1)
    out_ref[...] = jnp.where(jnp.abs(a - b) <= 31, rolled, 0.0)


def pack_rows(rep_ref, rows_ref, blend_ref, route_ref, line_ref, *refs):
    out_refs, (split_ref, hot_ref) = refs[:OWNERS], refs[OWNERS:]
    chunks = rows_ref.shape[0] // LANES
    blend = blend_ref[...]
    route = route_ref[...]
    line = line_ref[...]
    i = lax.broadcasted_iota(jnp.int32, (LANES, LANES), 0)
    j = lax.broadcasted_iota(jnp.int32, (LANES, LANES), 1)
    upto = (i <= j).astype(BF16)
    ones = jnp.ones((LANES, LANES), BF16)
    ci = lax.broadcasted_iota(jnp.int32, (16, 16), 0)
    cj = lax.broadcasted_iota(jnp.int32, (16, 16), 1)
    before = (cj < ci).astype(BF16)
    key = route * CAPACITY
    for owner in range(OWNERS):
        mine = (route == owner).astype(F32)
        mine16 = jnp.concatenate([mine, jnp.zeros((16 - chunks, LANES), F32)], axis=0).astype(BF16)
        upto_here = jnp.dot(mine16, upto, preferred_element_type=F32)
        totals = jnp.dot(mine16, ones, preferred_element_type=F32).astype(BF16)
        offset = jnp.dot(before, totals, preferred_element_type=F32)
        rank = (upto_here + offset)[:chunks] - 1.0
        key = key + jnp.where(route == owner, rank, 0.0).astype(jnp.int32)
    square = jnp.concatenate([blend, jnp.zeros((LANES - chunks, LANES), F32)], axis=0)
    columns = square.T
    for c in range(chunks):
        weighted = rows_ref[c * LANES : (c + 1) * LANES, :] * columns[:, c : c + 1]
        high, low = halves(weighted)
        split_ref[c * LANES : (c + 1) * LANES, :LANES] = high
        split_ref[c * LANES : (c + 1) * LANES, LANES:] = low
    first, second, third = thirds(blend)
    upper = line // 32
    parts = [first, second, third, upper.astype(BF16), (line - upper * 32).astype(BF16)]
    notes = jnp.concatenate(
        [
            jnp.concatenate(
                [p.astype(F32)[c : c + 1] for p in parts] + [jnp.zeros((3, LANES), F32)], axis=0
            )
            for c in range(chunks)
        ],
        axis=1,
    ).astype(BF16)
    for step, out_ref in enumerate(out_refs):
        owner = (rep_ref[0] + step) % OWNERS
        slot = lax.broadcasted_iota(jnp.int32, (CAPACITY, LANES), 0) + owner * CAPACITY
        for c in range(chunks):
            hot = jnp.where(slot == key[c : c + 1, :], 1.0, 0.0)
            hot_ref[:, c * LANES : (c + 1) * LANES] = hot.astype(BF16)
        hot = hot_ref[...]
        both = jnp.dot(hot, split_ref[...], preferred_element_type=F32)
        out_ref[:CAPACITY, :] = both[:, :LANES] + both[:, LANES:]
        meta = lax.dot_general(
            notes, hot, (((1,), (1,)), ((), ())), preferred_element_type=F32
        )
        weight = meta[0:1] + meta[1:2] + meta[2:3]
        where = meta[3:4] * 32.0 + meta[4:5]
        out_ref[CAPACITY:, :] = jnp.concatenate(
            [weight[:, q * LANES : (q + 1) * LANES] for q in range(4)]
            + [where[:, q * LANES : (q + 1) * LANES] for q in range(4)],
            axis=0,
        )


def line_sums(got_ref, hot_ref):
    at = lax.broadcasted_iota(jnp.int32, (LINES, LANES), 0)
    meta = got_ref[CAPACITY:, :]
    where = meta[4:8].astype(jnp.int32)
    for q in range(4):
        hot = jnp.where(at == where[q : q + 1, :], 1.0, 0.0)
        hot_ref[:, q * LANES : (q + 1) * LANES] = hot.astype(BF16)
    hot = hot_ref[...]
    high, low = halves(got_ref[:CAPACITY, :])
    rows = jnp.dot(hot, jnp.concatenate([high, low], axis=1), preferred_element_type=F32)
    weight = jnp.concatenate([meta[q : q + 1] for q in range(4)], axis=1)
    parts = [p.astype(F32) for p in thirds(weight)]
    stacked = jnp.concatenate(parts + [jnp.zeros((5, CAPACITY), F32)], axis=0).astype(BF16)
    weights = lax.dot_general(hot, stacked, (((1,), (1,)), ((), ())), preferred_element_type=F32)
    return rows[:, :LANES] + rows[:, LANES:], weights[:, 0:1] + weights[:, 1:2] + weights[:, 2:3]


def begin_sums(got_ref, total_ref, weight_ref, hot_ref):
    total_ref[...], weight_ref[...] = line_sums(got_ref, hot_ref)


def add_sums(got_ref, before_ref, before_weight_ref, total_ref, weight_ref, hot_ref):
    rows, weights = line_sums(got_ref, hot_ref)
    total_ref[...] = before_ref[...] + rows
    weight_ref[...] = before_weight_ref[...] + weights


def observe(got_ref, before_ref, before_weight_ref, out_ref, hot_ref, plane_ref):
    rows, weights = line_sums(got_ref, hot_ref)
    plane_ref[...] = (before_ref[...] + rows) / (before_weight_ref[...] + weights)
    store_tiles(plane_ref, out_ref)


def columns_from(got_ref, out_ref):
    for i in range(8):
        turned = got_ref[pl.ds(i, Z, stride=8), :].T
        for j in range(4):
            out_ref[SIDE * (8 * j + i) : SIDE * (8 * j + i) + SIDE, :] = turned[SIDE * j : SIDE * j + SIDE, :]


def store_edges(side_ref, out_ref, own_ref, other_ref, rows=SIDE, rim=RIM):
    skip = (SIDE - rim) * rows
    own_ref[...] = out_ref[pl.ds(pl.multiple_of(side_ref[0] * skip, 8), rim * rows), :]
    other_ref[...] = out_ref[pl.ds(pl.multiple_of((1 - side_ref[0]) * skip, 8), rim * rows), :]


def swap_leading(in_ref, out_ref):
    for i in range(SIDE):
        out_ref[SIDE * i : SIDE * i + SIDE, :] = in_ref[pl.ds(i, SIDE, stride=SIDE), :]


def arrive(side_ref, got_ref, out_ref, swapped_ref, own_ref, other_ref):
    columns_from(got_ref, out_ref)
    swap_leading(out_ref, swapped_ref)
    store_edges(side_ref, swapped_ref, own_ref, other_ref)


def taps_of(taps_ref, flip):
    return [taps_ref[TAPS - 1 - k if flip else k] for k in range(TAPS)]


def correlate(taps, in_ref, cells, leads, rows, shift, store):
    def block(index, carry):
        row = index * 8
        for first in range(0, leads, 8):
            totals = [None] * 8
            for cell in range(max(0, first - shift), min(cells, first + 7 + TAPS - shift)):
                value = in_ref[pl.ds(pl.multiple_of(cell * rows + row, 8), 8), :]
                for i in range(8):
                    k = cell - first - i + shift
                    if 0 <= k < TAPS:
                        term = taps[k] * value
                        totals[i] = term if totals[i] is None else totals[i] + term
            for i in range(8):
                store(first + i, row, jnp.zeros((8, Z), F32) if totals[i] is None else totals[i])
        return carry

    lax.fori_loop(0, rows // 8, block, 0)


def own_share(flip, leads, rows, shift, taps_ref, mid_ref, out_ref):
    def store(lead, row, value):
        out_ref[pl.ds(pl.multiple_of(lead * rows + row, 8), 8), :] = value

    correlate(taps_of(taps_ref, flip), mid_ref, SIDE, leads, rows, shift, store)


def add_rims(taps_ref, flip, side_ref, part_ref, near_ref, far_ref, store, rows=SIDE):
    taps = taps_of(taps_ref, flip)
    side = side_ref[0]
    for row in range(0, rows, 8):
        near = [near_ref[rows * i + row : rows * i + row + 8, :] for i in range(RIM)]
        far = [far_ref[rows * i + row : rows * i + row + 8, :] for i in range(RIM)]
        low = [jnp.where(side == 0, a, b) for a, b in zip(near, far, strict=True)]
        high = [jnp.where(side == 0, b, a) for a, b in zip(near, far, strict=True)]
        for lead in range(SIDE):
            total = part_ref[rows * lead + row : rows * lead + row + 8, :]
            for i in range(RIM):
                if i >= lead:
                    total = total + taps[i - lead] * low[i]
                if i <= lead - SIDE + RIM:
                    total = total + taps[SIDE + RIM + i - lead] * high[i]
            store(lead, row, total)


def swapped(lead, row):
    return pl.ds(SIDE * row + lead, 8, stride=SIDE)


def along_y_first(taps_ref, side_ref, part_ref, near_ref, far_ref, out_ref, cross_ref, pair_ref):
    def store(lead, row, value):
        out_ref[swapped(lead, row), :] = value

    add_rims(taps_ref, False, side_ref, part_ref, near_ref, far_ref, store)
    store_edges(side_ref, out_ref, cross_ref, pair_ref)


def extend(side_ref, tile_ref, near_ref, far_ref, out_ref):
    zeros = jnp.zeros((8, Z), F32)
    for x in range(SIDE):
        out_ref[WIDE * x : WIDE * x + 8, :] = zeros
        out_ref[WIDE * x + WIDE - 8 : WIDE * x + WIDE, :] = zeros
        out_ref[WIDE * x + MARGIN : WIDE * x + MARGIN + SIDE, :] = tile_ref[SIDE * x : SIDE * x + SIDE, :]
    for r in range(RIM):
        for x in range(0, SIDE, 8):
            near = near_ref[SIDE * r + x : SIDE * r + x + 8, :]
            far = far_ref[SIDE * r + x : SIDE * r + x + 8, :]
            below = pl.ds(WIDE * x + r + 1, 8, stride=WIDE)
            above = pl.ds(WIDE * x + MARGIN + SIDE + r, 8, stride=WIDE)
            out_ref[below, :] = jnp.where(side_ref[0] == 0, near, far)
            out_ref[above, :] = jnp.where(side_ref[0] == 0, far, near)


def rim_share(taps, upper, rim_ref, row):
    cells = [rim_ref[SIDE * i + row : SIDE * i + row + 8, :] for i in range(2 * RIM)]
    for n in range(2 * RIM):
        used = range(n + 1) if upper else range(n, 2 * RIM)
        total = None
        for i in used:
            term = taps[2 * RIM + i - n if upper else i - n] * cells[i]
            total = term if total is None else total + term
        yield n, total


def near_share(taps_ref, side_ref, rim_ref, out_ref):
    taps = taps_of(taps_ref, True)
    for side in range(2):

        @pl.when(side_ref[0] == side)
        def _():
            for row in range(0, SIDE, 8):
                for n, total in rim_share(taps, side == 1, rim_ref, row):
                    out_ref[SIDE * n + row : SIDE * n + row + 8, :] = total


def wide_rows(taps_ref, side_ref, part_ref, near_ref, far_ref, out_ref, cross_ref, pair_ref):
    taps = taps_of(taps_ref, True)
    for side in range(2):

        @pl.when(side_ref[0] == side)
        def _():
            for row in range(0, SIDE, 8):

                def store(e, total):
                    out_ref[pl.ds(WIDE * row + e, 8, stride=WIDE), :] = (
                        part_ref[SIDE * e + row : SIDE * e + row + 8, :] + total
                    )

                for n, total in rim_share(taps, side == 0, far_ref, row):
                    share = near_ref[SIDE * n + row : SIDE * n + row + 8, :]
                    store(1 + n, share if side == 0 else total)
                    store(SIDE + 1 + n, total if side == 0 else share)
                for e in (0, SIDE - 1, SIDE, WIDE - 1):
                    store(e, 0.0)

    store_edges(side_ref, out_ref, cross_ref, pair_ref, WIDE)


def update_wide(
    taps_ref,
    side_ref,
    part_ref,
    cross_ref,
    pair_ref,
    start_ref,
    new_ref,
    out_ref,
    cross_out_ref,
    pair_out_ref,
    turned_ref,
):
    def store(x, e, value):
        spot = slice(WIDE * x + e, WIDE * x + e + 8)
        new = start_ref[spot, :] * value
        new_ref[spot, :] = new
        turned_ref[pl.ds(SIDE * e + x, 8, stride=SIDE), :] = new

    add_rims(taps_ref, True, side_ref, part_ref, cross_ref, pair_ref, store, WIDE)

    def store_y(y, x, value):
        out_ref[swapped(y, x), :] = value

    correlate(taps_of(taps_ref, False), turned_ref, WIDE, SIDE, SIDE, RIM - MARGIN, store_y)
    store_edges(side_ref, out_ref, cross_out_ref, pair_out_ref, rim=2 * RIM)


def axial(value, band, back):
    dims = (((1,), (0 if back else 1,)), ((), ()))
    high, low = halves(value)
    band_high, band_low = halves(band)
    double = jnp.concatenate([band_high, band_high], axis=0 if back else 1)
    both = jnp.concatenate([high, low], axis=1)
    return lax.dot_general(both, double, dims, preferred_element_type=F32) + lax.dot_general(
        high, band_low, dims, preferred_element_type=F32
    )


def along_x_last(taps_ref, side_ref, part_ref, cross_ref, pair_ref, cols_ref):
    def store(lead, row, value):
        cols_ref[SIDE * lead + row : SIDE * lead + row + 8, :] = value

    add_rims(taps_ref, False, side_ref, part_ref, cross_ref, pair_ref, store)


def blur(taps_ref, side_ref, part_ref, cross_ref, pair_ref, band_ref, out_ref, cols_ref):
    along_x_last(taps_ref, side_ref, part_ref, cross_ref, pair_ref, cols_ref)
    out_ref[...] = axial(cols_ref[...], band_ref[...], False)


def first_ratio(
    side_ref,
    got_ref,
    blurred_ref,
    band_ref,
    seen_ref,
    cross_ref,
    pair_ref,
    out_ref,
    own_ref,
    other_ref,
    cols_ref,
):
    columns_from(got_ref, seen_ref)
    cols_ref[...] = axial(seen_ref[...] / blurred_ref[...], band_ref[...], True)
    swap_leading(cols_ref, out_ref)
    store_edges(side_ref, out_ref, own_ref, other_ref, rim=2 * RIM)
    store_edges(side_ref, seen_ref, cross_ref, pair_ref)


def extend_x(side_ref, tile_ref, cross_ref, pair_ref, out_ref):
    ones = jnp.ones((SIDE, Z), F32)
    out_ref[:SIDE, :] = ones
    out_ref[SIDE * (WIDE - 1) :, :] = ones
    out_ref[SIDE * MARGIN : SIDE * (MARGIN + SIDE), :] = tile_ref[...]
    low_at, high_at = SIDE, SIDE * (MARGIN + SIDE)
    cross_at = pl.multiple_of(jnp.where(side_ref[0] == 0, low_at, high_at), 8)
    pair_at = pl.multiple_of(jnp.where(side_ref[0] == 0, high_at, low_at), 8)
    out_ref[pl.ds(cross_at, RIM * SIDE), :] = cross_ref[...]
    out_ref[pl.ds(pair_at, RIM * SIDE), :] = pair_ref[...]


def blur_ratio(
    taps_ref,
    side_ref,
    part_ref,
    cross_ref,
    pair_ref,
    band_ref,
    seen_ref,
    out_ref,
    own_ref,
    other_ref,
    cols_ref,
    ratio_ref,
):
    taps = taps_of(taps_ref, False)
    for side in range(2):

        @pl.when(side_ref[0] == side)
        def _():
            for row in range(0, SIDE, 8):

                def store(e, total):
                    spot = slice(SIDE * e + row, SIDE * e + row + 8)
                    cols_ref[spot, :] = part_ref[spot, :] + total

                low_ref, high_ref = (cross_ref, pair_ref) if side == 0 else (pair_ref, cross_ref)
                for n, total in rim_share(taps, False, low_ref, row):
                    store(1 + n, total)
                for n, total in rim_share(taps, True, high_ref, row):
                    store(SIDE + 1 + n, total)
                for e in (0, SIDE - 1, SIDE, WIDE - 1):
                    store(e, 1.0 if e in (0, WIDE - 1) else 0.0)

    band = band_ref[...]
    for start in range(0, WIDE * SIDE, 256):
        spot = slice(start, start + 256)
        ratio = seen_ref[spot, :] / axial(cols_ref[spot, :], band, False)
        ratio_ref[spot, :] = axial(ratio, band, True)

    def store_x(x, y, value):
        out_ref[swapped(x, y), :] = value

    correlate(taps_of(taps_ref, True), ratio_ref, WIDE, SIDE, SIDE, RIM - MARGIN, store_x)
    store_edges(side_ref, out_ref, own_ref, other_ref)


def last_update(taps_ref, side_ref, part_ref, near_ref, far_ref, estimate_ref, out_ref, cols_ref):
    def store(lead, row, value):
        cols_ref[swapped(lead, row), :] = value

    add_rims(taps_ref, True, side_ref, part_ref, near_ref, far_ref, store)
    for i in range(8):
        block = jnp.concatenate(
            [
                estimate_ref[WIDE * x + MARGIN : WIDE * x + MARGIN + SIDE, :]
                * cols_ref[SIDE * x : SIDE * x + SIDE, :]
                for x in range(i, SIDE, 8)
            ],
            axis=0,
        )
        out_ref[pl.ds(i, Z, stride=8), :] = block.T


FLAT = (SIDE * SIDE, Z)
EDGE = (RIM * SIDE, Z)
WIDE_FLAT = (SIDE * WIDE, Z)
WIDE_EDGE = (RIM * WIDE, Z)
WIDE_RIM = (2 * RIM * SIDE, Z)
PIECES = (Z, 8, LANES)


def shards(camera_rows, blend, route, line, start, psf_xy, psf_z):
    slabs, reps = lax.axis_size("slab"), lax.axis_size("rep")
    x_tiles = LINES // SIDE
    y_tiles = slabs // x_tiles
    chunks = camera_rows.shape[0] // LANES
    pair_swaps = [(t, t ^ 1) for t in range(slabs)]
    cross_swaps = []
    for t in range(1, slabs, 2):
        if t % x_tiles != x_tiles - 1:
            cross_swaps += [(t, t + 1), (t + 1, t)]
    side = (lax.axis_index("slab") % 2).reshape(1)
    y_pairs = []
    for t in range(slabs):
        for r in range(reps):
            y = r * y_tiles + t // x_tiles + 1
            if y < y_tiles * reps:
                up = (y % y_tiles) * x_tiles + t % x_tiles
                y_pairs.append((t * reps + r, up * reps + y // y_tiles))

    def rims_x(cross, pair):
        return lax.ppermute(cross, "slab", cross_swaps), lax.ppermute(pair, "slab", pair_swaps)

    y_one, y_two = [], []
    for low, high in y_pairs:
        upward, downward = (y_one, y_two) if (low // reps) % 2 == 0 else (y_two, y_one)
        upward.append((low, high))
        downward.append((high, low))

    def rims_y(own, other):
        axes = ("slab", "rep")
        return lax.ppermute(other, axes, y_one), lax.ppermute(own, axes, y_two)

    def turn(pieces):
        return lax.all_to_all(pieces, "slab", split_axis=0, concat_axis=0, tiled=True)

    taps = psf_xy / jnp.sum(psf_xy)

    arrived = turn(call(store_tiles, [PIECES], [], start.reshape(LINES, LANES))[0])
    band = call(axial_band, [(Z, LANES)], [((8, LANES), F32)], psf_z[None, :])[0]
    sent = call(
        pack_rows,
        [(CAPACITY + META, LANES)] * OWNERS,
        [((chunks * LANES, 2 * LANES), BF16), ((CAPACITY, chunks * LANES), BF16)],
        lax.axis_index("rep").reshape(1),
        camera_rows,
        blend.reshape(chunks, LANES),
        route.reshape(chunks, LANES),
        line.reshape(chunks, LANES),
        smem=1,
    )
    got = [
        block if step == 0 else lax.ppermute(block, "rep", [(r, (r + step) % reps) for r in range(reps)])
        for step, block in enumerate(sent)
    ]
    hot = [((LINES, CAPACITY), BF16)]
    sums = call(begin_sums, [(LINES, LANES), (LINES, 1)], hot, got[0])
    for block in got[1:-1]:
        sums = call(add_sums, [(LINES, LANES), (LINES, 1)], hot, block, *sums)
    seen_pieces = call(observe, [PIECES], hot + [((LINES, LANES), F32)], got[-1], *sums)[0]
    arrived, seen_pieces = lax.optimization_barrier((arrived, seen_pieces))
    estimate, flipped, *edges = call(
        arrive, [FLAT, FLAT, EDGE, EDGE], [], side, arrived.reshape(Z * 8, LANES), smem=1
    )
    seen_arrived = turn(seen_pieces)

    def own(flip, value, rows=SIDE):
        kernel = functools.partial(own_share, flip, SIDE, rows, RIM)
        return call(kernel, [(SIDE * rows, Z)], [], taps, value, smem=1)[0]

    cols = [(FLAT, F32)]
    start_rims = rims_y(*edges)
    value, *edges = call(
        along_y_first, [FLAT, EDGE, EDGE], [], taps, side, own(False, flipped), *start_rims, smem=2
    )
    blurred = call(blur, [FLAT], cols, taps, side, own(False, value), *rims_x(*edges), band, smem=2)[0]
    seen, seen_cross, seen_pair, back, *edges = call(
        first_ratio,
        [FLAT, EDGE, EDGE, FLAT, WIDE_RIM, WIDE_RIM],
        cols,
        side,
        seen_arrived.reshape(Z * 8, LANES),
        blurred,
        band,
        smem=1,
    )

    def wide_own(flip, value):
        kernel = functools.partial(own_share, flip, WIDE, SIDE, RIM + MARGIN)
        return call(kernel, [WIDE_FLAT], [], taps, value, smem=1)[0]

    near, far = rims_y(*edges)
    part = wide_own(True, back)
    seen_cross, seen_pair, part = lax.optimization_barrier((seen_cross, seen_pair, part))
    near, *seen_rims = lax.optimization_barrier((near, *rims_x(seen_cross, seen_pair)))
    near = call(near_share, [WIDE_RIM], [], taps, side, near, smem=2)[0]
    value, *edges = call(
        wide_rows, [WIDE_FLAT, WIDE_EDGE, WIDE_EDGE], [], taps, side, part, near, far, smem=2
    )
    rims = rims_x(*edges)
    wide = call(extend, [WIDE_FLAT], [], side, estimate, *start_rims, smem=1)[0]
    wide, value, *edges = call(
        update_wide,
        [WIDE_FLAT, FLAT, WIDE_RIM, WIDE_RIM],
        [(WIDE_FLAT, F32)],
        taps,
        side,
        own(True, value, WIDE),
        *rims,
        wide,
        smem=2,
    )
    rims = rims_x(*edges)
    seen = call(extend_x, [WIDE_FLAT], [], side, seen, *seen_rims, smem=1)[0]
    value, *edges = call(
        blur_ratio,
        [FLAT, EDGE, EDGE],
        [(WIDE_FLAT, F32), (WIDE_FLAT, F32)],
        taps,
        side,
        wide_own(False, value),
        *rims,
        band,
        seen,
        smem=2,
    )
    rims = rims_y(*edges)
    pieces = call(
        last_update, [(Z * 8, LANES)], cols, taps, side, own(True, value), *rims, wide, smem=2
    )[0]
    done = turn(pieces.reshape(PIECES))
    plane = call(plane_of, [(LINES, LANES)], [], done)[0]
    return plane.reshape(1, LINES, LANES)


def solution(mesh):
    in_specs = (
        P(("slab", "rep"), None),
        P(("slab", "rep")),
        P(("slab", "rep")),
        P(("slab", "rep")),
        P("slab", None, "rep"),
        P(),
        P(),
    )
    out_specs = P("slab", None, "rep")
    return jax.shard_map(shards, mesh=mesh, in_specs=in_specs, out_specs=out_specs, check_vma=False)
```

```python
import functools

import jax
import jax.numpy as jnp
from jax import lax
from jax.experimental import pallas as pl
from jax.experimental.pallas import tpu as pltpu
from jax.sharding import PartitionSpec as P

F32 = jnp.float32
BF16 = jnp.bfloat16
LANES = 128
SIDE = 32
TAPS = 31
RIM = TAPS // 2
WIDE = 64
MARGIN = 16
OWNERS = 4
CAPACITY = 512
META = 8
LINES = 1024
Z = 128
VMEM_LIMIT = 40 * 1024 * 1024


def call(kernel, out_shapes, scratch, *args, smem=0):
    specs = [
        pl.BlockSpec(memory_space=pltpu.SMEM if i < smem else pltpu.VMEM)
        for i in range(len(args))
    ]
    outs = tuple(jax.ShapeDtypeStruct(s, F32) for s in out_shapes)
    return pl.pallas_call(
        kernel,
        out_shape=outs,
        in_specs=specs,
        out_specs=tuple(pl.BlockSpec(memory_space=pltpu.VMEM) for _ in outs),
        scratch_shapes=[pltpu.VMEM(s, d) for s, d in scratch],
        compiler_params=pltpu.CompilerParams(vmem_limit_bytes=VMEM_LIMIT),
        name=kernel.func.__name__ if isinstance(kernel, functools.partial) else kernel.__name__,
    )(*args)


def halves(value):
    high = value.astype(BF16)
    return high, (value - high.astype(F32)).astype(BF16)


def thirds(value):
    high, rest = halves(value)
    low = (value - high.astype(F32) - rest.astype(F32)).astype(BF16)
    return high, rest, low


def swap_lanes(pairs, first, moves):
    mixed = [jnp.where(first, b, a) for a, b in pairs]
    up = [pltpu.roll(m, moves[0], axis=1) for m in mixed]
    down = up if moves[0] == moves[1] else [pltpu.roll(m, moves[1], axis=1) for m in mixed]
    return [
        (jnp.where(first, a, u), jnp.where(first, d, b)) for (a, b), u, d in zip(pairs, up, down, strict=True)
    ]


def lane_blocks(pieces):
    lane = lax.broadcasted_iota(jnp.int32, (8, LANES), 1)
    outer = swap_lanes([pair for a, b, c, d in pieces for pair in ((a, c), (b, d))], lane < 64, (64, 64))
    rows = [(ac[0], bd[0], ac[1], bd[1]) for ac, bd in zip(outer[::2], outer[1::2], strict=True)]
    inner = swap_lanes([pair for a, b, c, d in rows for pair in ((a, b), (c, d))], lane % 64 < 32, (32, 96))
    return [ab + cd for ab, cd in zip(inner[::2], inner[1::2], strict=True)]


def store_tiles(plane_ref, out_ref):
    for first in range(0, 32, 8):
        parts = range(first, first + 8)
        rows = [
            tuple(plane_ref[SIDE * p + 8 * j : SIDE * p + 8 * j + 8, :] for j in range(4)) for p in parts
        ]
        for part, piece in zip(parts, lane_blocks(rows), strict=True):
            for sub in range(4):
                out_ref[32 * sub + part] = piece[sub]


def plane_of(got_ref, out_ref):
    for first in range(0, 32, 8):
        parts = range(first, first + 8)
        pieces = [tuple(got_ref[32 * sub + p] for sub in range(4)) for p in parts]
        for part, rows in zip(parts, lane_blocks(pieces), strict=True):
            for j in range(4):
                out_ref[SIDE * part + 8 * j : SIDE * part + 8 * j + 8, :] = rows[j]


def axial_band(psf_ref, out_ref, row_ref):
    row_ref[...] = jnp.zeros((8, LANES), F32)
    row_ref[0:1, : psf_ref.shape[1]] = psf_ref[...]
    psf = row_ref[0:1, :]
    rows = jnp.broadcast_to(psf / jnp.sum(psf, axis=1, keepdims=True), (Z, LANES))
    rolled = pltpu.roll(rows, LANES - 31, axis=1, stride=1, stride_axis=0)
    a = lax.broadcasted_iota(jnp.int32, (Z, LANES), 0)
    b = lax.broadcasted_iota(jnp.int32, (Z, LANES), 1)
    out_ref[...] = jnp.where(jnp.abs(a - b) <= 31, rolled, 0.0)


def split_rows(rows_ref, blend, split_ref):
    chunks = blend.shape[0]
    columns = jnp.concatenate([blend, jnp.zeros((LANES - chunks, LANES), F32)], axis=0).T
    for c in range(chunks):
        high, low = halves(rows_ref[c * LANES : (c + 1) * LANES, :] * columns[:, c : c + 1])
        split_ref[c * LANES : (c + 1) * LANES, :LANES] = high
        split_ref[c * LANES : (c + 1) * LANES, LANES:] = low


def pack_rows(rep_ref, rows_ref, blend_ref, route_ref, line_ref, *refs):
    out_refs, (split_ref, hot_ref) = refs[: OWNERS - 1], refs[OWNERS - 1 :]
    chunks = rows_ref.shape[0] // LANES
    blend = blend_ref[...]
    route = route_ref[...]
    line = line_ref[...]
    i = lax.broadcasted_iota(jnp.int32, (LANES, LANES), 0)
    j = lax.broadcasted_iota(jnp.int32, (LANES, LANES), 1)
    upto = (i <= j).astype(BF16)
    ones = jnp.ones((LANES, LANES), BF16)
    ci = lax.broadcasted_iota(jnp.int32, (16, 16), 0)
    cj = lax.broadcasted_iota(jnp.int32, (16, 16), 1)
    before = (cj < ci).astype(BF16)
    key = route * CAPACITY
    for owner in range(OWNERS):
        mine = (route == owner).astype(F32)
        mine16 = jnp.concatenate([mine, jnp.zeros((16 - chunks, LANES), F32)], axis=0).astype(BF16)
        upto_here = jnp.dot(mine16, upto, preferred_element_type=F32)
        totals = jnp.dot(mine16, ones, preferred_element_type=F32).astype(BF16)
        offset = jnp.dot(before, totals, preferred_element_type=F32)
        rank = (upto_here + offset)[:chunks] - 1.0
        key = key + jnp.where(route == owner, rank, 0.0).astype(jnp.int32)
    split_rows(rows_ref, blend, split_ref)
    first, second, third = thirds(blend)
    upper = line // 32
    parts = [first, second, third, upper.astype(BF16), (line - upper * 32).astype(BF16)]
    notes = jnp.concatenate(
        [
            jnp.concatenate(
                [p.astype(F32)[c : c + 1] for p in parts] + [jnp.zeros((3, LANES), F32)], axis=0
            )
            for c in range(chunks)
        ],
        axis=1,
    ).astype(BF16)
    for step, out_ref in enumerate(out_refs, 1):
        owner = (rep_ref[0] + step) % OWNERS
        slot = lax.broadcasted_iota(jnp.int32, (CAPACITY, LANES), 0) + owner * CAPACITY
        for c in range(chunks):
            hot = jnp.where(slot == key[c : c + 1, :], 1.0, 0.0)
            hot_ref[:, c * LANES : (c + 1) * LANES] = hot.astype(BF16)
        hot = hot_ref[...]
        both = jnp.dot(hot, split_ref[...], preferred_element_type=F32)
        out_ref[:CAPACITY, :] = both[:, :LANES] + both[:, LANES:]
        meta = lax.dot_general(
            notes, hot, (((1,), (1,)), ((), ())), preferred_element_type=F32
        )
        weight = meta[0:1] + meta[1:2] + meta[2:3]
        where = meta[3:4] * 32.0 + meta[4:5]
        out_ref[CAPACITY:, :] = jnp.concatenate(
            [weight[:, q * LANES : (q + 1) * LANES] for q in range(4)]
            + [where[:, q * LANES : (q + 1) * LANES] for q in range(4)],
            axis=0,
        )


def line_sums(got_ref, hot_ref):
    at = lax.broadcasted_iota(jnp.int32, (LINES, LANES), 0)
    meta = got_ref[CAPACITY:, :]
    where = meta[4:8].astype(jnp.int32)
    for q in range(4):
        hot = jnp.where(at == where[q : q + 1, :], 1.0, 0.0)
        hot_ref[:, q * LANES : (q + 1) * LANES] = hot.astype(BF16)
    hot = hot_ref[...]
    high, low = halves(got_ref[:CAPACITY, :])
    rows = jnp.dot(hot, jnp.concatenate([high, low], axis=1), preferred_element_type=F32)
    weight = jnp.concatenate([meta[q : q + 1] for q in range(4)], axis=1)
    parts = [p.astype(F32) for p in thirds(weight)]
    stacked = jnp.concatenate(parts + [jnp.zeros((5, CAPACITY), F32)], axis=0).astype(BF16)
    weights = lax.dot_general(hot, stacked, (((1,), (1,)), ((), ())), preferred_element_type=F32)
    return rows[:, :LANES] + rows[:, LANES:], weights[:, 0:1] + weights[:, 1:2] + weights[:, 2:3]


def begin_sums(rep_ref, rows_ref, blend_ref, route_ref, line_ref, total_ref, weight_ref, split_ref, hot_ref):
    blend = blend_ref[...]
    chunks = blend.shape[0]
    split_rows(rows_ref, blend, split_ref)
    where = jnp.where(route_ref[...] == rep_ref[0], line_ref[...], -1)
    at = lax.broadcasted_iota(jnp.int32, (LINES, LANES), 0)
    for c in range(chunks):
        hot = jnp.where(at == where[c : c + 1, :], 1.0, 0.0)
        hot_ref[:, c * LANES : (c + 1) * LANES] = hot.astype(BF16)
    hot = hot_ref[...]
    rows = jnp.dot(hot, split_ref[...], preferred_element_type=F32)
    parts = [
        jnp.concatenate([p.astype(F32)[c : c + 1] for c in range(chunks)], axis=1) for p in thirds(blend)
    ]
    stacked = jnp.concatenate(parts + [jnp.zeros((5, chunks * LANES), F32)], axis=0).astype(BF16)
    weights = lax.dot_general(hot, stacked, (((1,), (1,)), ((), ())), preferred_element_type=F32)
    total_ref[...] = rows[:, :LANES] + rows[:, LANES:]
    weight_ref[...] = weights[:, 0:1] + weights[:, 1:2] + weights[:, 2:3]


def add_sums(got_ref, before_ref, before_weight_ref, total_ref, weight_ref, hot_ref):
    rows, weights = line_sums(got_ref, hot_ref)
    total_ref[...] = before_ref[...] + rows
    weight_ref[...] = before_weight_ref[...] + weights


def observe(got_ref, before_ref, before_weight_ref, out_ref, hot_ref, plane_ref):
    rows, weights = line_sums(got_ref, hot_ref)
    plane_ref[...] = (before_ref[...] + rows) / (before_weight_ref[...] + weights)
    store_tiles(plane_ref, out_ref)


def columns_from(got_ref, out_ref):
    for i in range(8):
        turned = got_ref[pl.ds(i, Z, stride=8), :].T
        for j in range(4):
            out_ref[SIDE * (8 * j + i) : SIDE * (8 * j + i) + SIDE, :] = turned[SIDE * j : SIDE * j + SIDE, :]


def store_edges(side_ref, out_ref, own_ref, other_ref, rows=SIDE, rim=RIM):
    skip = (SIDE - rim) * rows
    own_ref[...] = out_ref[pl.ds(pl.multiple_of(side_ref[0] * skip, 8), rim * rows), :]
    other_ref[...] = out_ref[pl.ds(pl.multiple_of((1 - side_ref[0]) * skip, 8), rim * rows), :]


def swap_leading(in_ref, out_ref):
    for i in range(SIDE):
        out_ref[SIDE * i : SIDE * i + SIDE, :] = in_ref[pl.ds(i, SIDE, stride=SIDE), :]


def arrive(side_ref, got_ref, out_ref, swapped_ref, own_ref, other_ref):
    columns_from(got_ref, out_ref)
    swap_leading(out_ref, swapped_ref)
    store_edges(side_ref, swapped_ref, own_ref, other_ref)


def taps_of(taps_ref, flip):
    return [taps_ref[TAPS - 1 - k if flip else k] for k in range(TAPS)]


def correlate(taps, in_ref, cells, leads, rows, shift, store):
    def block(index, carry):
        row = index * 8
        for first in range(0, leads, 8):
            totals = [None] * 8
            for cell in range(max(0, first - shift), min(cells, first + 7 + TAPS - shift)):
                value = in_ref[pl.ds(pl.multiple_of(cell * rows + row, 8), 8), :]
                for i in range(8):
                    k = cell - first - i + shift
                    if 0 <= k < TAPS:
                        term = taps[k] * value
                        totals[i] = term if totals[i] is None else totals[i] + term
            for i in range(8):
                store(first + i, row, jnp.zeros((8, Z), F32) if totals[i] is None else totals[i])
        return carry

    lax.fori_loop(0, rows // 8, block, 0)


def own_share(flip, leads, rows, shift, taps_ref, mid_ref, out_ref):
    def store(lead, row, value):
        out_ref[pl.ds(pl.multiple_of(lead * rows + row, 8), 8), :] = value

    correlate(taps_of(taps_ref, flip), mid_ref, SIDE, leads, rows, shift, store)


def add_rims(taps_ref, flip, side_ref, part_ref, near_ref, far_ref, store, rows=SIDE):
    taps = taps_of(taps_ref, flip)
    side = side_ref[0]
    for row in range(0, rows, 8):
        near = [near_ref[rows * i + row : rows * i + row + 8, :] for i in range(RIM)]
        far = [far_ref[rows * i + row : rows * i + row + 8, :] for i in range(RIM)]
        low = [jnp.where(side == 0, a, b) for a, b in zip(near, far, strict=True)]
        high = [jnp.where(side == 0, b, a) for a, b in zip(near, far, strict=True)]
        for lead in range(SIDE):
            total = part_ref[rows * lead + row : rows * lead + row + 8, :]
            for i in range(RIM):
                if i >= lead:
                    total = total + taps[i - lead] * low[i]
                if i <= lead - SIDE + RIM:
                    total = total + taps[SIDE + RIM + i - lead] * high[i]
            store(lead, row, total)


def swapped(lead, row):
    return pl.ds(SIDE * row + lead, 8, stride=SIDE)


def along_y_first(taps_ref, side_ref, part_ref, near_ref, far_ref, out_ref, cross_ref, pair_ref):
    def store(lead, row, value):
        out_ref[swapped(lead, row), :] = value

    add_rims(taps_ref, False, side_ref, part_ref, near_ref, far_ref, store)
    store_edges(side_ref, out_ref, cross_ref, pair_ref)


def extend(side_ref, tile_ref, near_ref, far_ref, out_ref):
    zeros = jnp.zeros((8, Z), F32)
    for x in range(SIDE):
        out_ref[WIDE * x : WIDE * x + 8, :] = zeros
        out_ref[WIDE * x + WIDE - 8 : WIDE * x + WIDE, :] = zeros
        out_ref[WIDE * x + MARGIN : WIDE * x + MARGIN + SIDE, :] = tile_ref[SIDE * x : SIDE * x + SIDE, :]
    for r in range(RIM):
        for x in range(0, SIDE, 8):
            near = near_ref[SIDE * r + x : SIDE * r + x + 8, :]
            far = far_ref[SIDE * r + x : SIDE * r + x + 8, :]
            below = pl.ds(WIDE * x + r + 1, 8, stride=WIDE)
            above = pl.ds(WIDE * x + MARGIN + SIDE + r, 8, stride=WIDE)
            out_ref[below, :] = jnp.where(side_ref[0] == 0, near, far)
            out_ref[above, :] = jnp.where(side_ref[0] == 0, far, near)


def rim_share(taps, upper, rim_ref, row):
    cells = [rim_ref[SIDE * i + row : SIDE * i + row + 8, :] for i in range(2 * RIM)]
    for n in range(2 * RIM):
        used = range(n + 1) if upper else range(n, 2 * RIM)
        total = None
        for i in used:
            term = taps[2 * RIM + i - n if upper else i - n] * cells[i]
            total = term if total is None else total + term
        yield n, total


def near_share(taps_ref, side_ref, rim_ref, out_ref):
    taps = taps_of(taps_ref, True)
    for side in range(2):

        @pl.when(side_ref[0] == side)
        def _():
            for row in range(0, SIDE, 8):
                for n, total in rim_share(taps, side == 1, rim_ref, row):
                    out_ref[SIDE * n + row : SIDE * n + row + 8, :] = total


def wide_rows(taps_ref, side_ref, part_ref, near_ref, far_ref, out_ref, cross_ref, pair_ref):
    taps = taps_of(taps_ref, True)
    for side in range(2):

        @pl.when(side_ref[0] == side)
        def _():
            for row in range(0, SIDE, 8):

                def store(e, total):
                    out_ref[pl.ds(WIDE * row + e, 8, stride=WIDE), :] = (
                        part_ref[SIDE * e + row : SIDE * e + row + 8, :] + total
                    )

                for n, total in rim_share(taps, side == 0, far_ref, row):
                    share = near_ref[SIDE * n + row : SIDE * n + row + 8, :]
                    store(1 + n, share if side == 0 else total)
                    store(SIDE + 1 + n, total if side == 0 else share)
                for e in (0, SIDE - 1, SIDE, WIDE - 1):
                    store(e, 0.0)

    store_edges(side_ref, out_ref, cross_ref, pair_ref, WIDE)


def update_wide(
    taps_ref,
    side_ref,
    part_ref,
    cross_ref,
    pair_ref,
    start_ref,
    new_ref,
    out_ref,
    cross_out_ref,
    pair_out_ref,
    turned_ref,
):
    def store(x, e, value):
        spot = slice(WIDE * x + e, WIDE * x + e + 8)
        new = start_ref[spot, :] * value
        new_ref[spot, :] = new
        turned_ref[pl.ds(SIDE * e + x, 8, stride=SIDE), :] = new

    add_rims(taps_ref, True, side_ref, part_ref, cross_ref, pair_ref, store, WIDE)

    def store_y(y, x, value):
        out_ref[swapped(y, x), :] = value

    correlate(taps_of(taps_ref, False), turned_ref, WIDE, SIDE, SIDE, RIM - MARGIN, store_y)
    store_edges(side_ref, out_ref, cross_out_ref, pair_out_ref, rim=2 * RIM)


def axial(value, band, back):
    dims = (((1,), (0 if back else 1,)), ((), ()))
    high, low = halves(value)
    band_high, band_low = halves(band)
    double = jnp.concatenate([band_high, band_high], axis=0 if back else 1)
    both = jnp.concatenate([high, low], axis=1)
    return lax.dot_general(both, double, dims, preferred_element_type=F32) + lax.dot_general(
        high, band_low, dims, preferred_element_type=F32
    )


def along_x_last(taps_ref, side_ref, part_ref, cross_ref, pair_ref, cols_ref):
    def store(lead, row, value):
        cols_ref[SIDE * lead + row : SIDE * lead + row + 8, :] = value

    add_rims(taps_ref, False, side_ref, part_ref, cross_ref, pair_ref, store)


def blur(taps_ref, side_ref, part_ref, cross_ref, pair_ref, band_ref, out_ref, cols_ref):
    along_x_last(taps_ref, side_ref, part_ref, cross_ref, pair_ref, cols_ref)
    out_ref[...] = axial(cols_ref[...], band_ref[...], False)


def first_ratio(
    side_ref,
    got_ref,
    blurred_ref,
    band_ref,
    seen_ref,
    cross_ref,
    pair_ref,
    out_ref,
    own_ref,
    other_ref,
    cols_ref,
):
    columns_from(got_ref, seen_ref)
    cols_ref[...] = axial(seen_ref[...] / blurred_ref[...], band_ref[...], True)
    swap_leading(cols_ref, out_ref)
    store_edges(side_ref, out_ref, own_ref, other_ref, rim=2 * RIM)
    store_edges(side_ref, seen_ref, cross_ref, pair_ref)


def extend_x(side_ref, tile_ref, cross_ref, pair_ref, out_ref):
    ones = jnp.ones((SIDE, Z), F32)
    out_ref[:SIDE, :] = ones
    out_ref[SIDE * (WIDE - 1) :, :] = ones
    out_ref[SIDE * MARGIN : SIDE * (MARGIN + SIDE), :] = tile_ref[...]
    low_at, high_at = SIDE, SIDE * (MARGIN + SIDE)
    cross_at = pl.multiple_of(jnp.where(side_ref[0] == 0, low_at, high_at), 8)
    pair_at = pl.multiple_of(jnp.where(side_ref[0] == 0, high_at, low_at), 8)
    out_ref[pl.ds(cross_at, RIM * SIDE), :] = cross_ref[...]
    out_ref[pl.ds(pair_at, RIM * SIDE), :] = pair_ref[...]


def blur_ratio(
    taps_ref,
    side_ref,
    part_ref,
    cross_ref,
    pair_ref,
    band_ref,
    seen_ref,
    out_ref,
    own_ref,
    other_ref,
    cols_ref,
    ratio_ref,
):
    taps = taps_of(taps_ref, False)
    for side in range(2):

        @pl.when(side_ref[0] == side)
        def _():
            for row in range(0, SIDE, 8):

                def store(e, total):
                    spot = slice(SIDE * e + row, SIDE * e + row + 8)
                    cols_ref[spot, :] = part_ref[spot, :] + total

                low_ref, high_ref = (cross_ref, pair_ref) if side == 0 else (pair_ref, cross_ref)
                for n, total in rim_share(taps, False, low_ref, row):
                    store(1 + n, total)
                for n, total in rim_share(taps, True, high_ref, row):
                    store(SIDE + 1 + n, total)
                for e in (0, SIDE - 1, SIDE, WIDE - 1):
                    store(e, 1.0 if e in (0, WIDE - 1) else 0.0)

    band = band_ref[...]
    for start in range(0, WIDE * SIDE, 256):
        spot = slice(start, start + 256)
        ratio = seen_ref[spot, :] / axial(cols_ref[spot, :], band, False)
        ratio_ref[spot, :] = axial(ratio, band, True)

    def store_x(x, y, value):
        out_ref[swapped(x, y), :] = value

    correlate(taps_of(taps_ref, True), ratio_ref, WIDE, SIDE, SIDE, RIM - MARGIN, store_x)
    store_edges(side_ref, out_ref, own_ref, other_ref)


def last_update(taps_ref, side_ref, part_ref, near_ref, far_ref, estimate_ref, out_ref, cols_ref):
    def store(lead, row, value):
        cols_ref[swapped(lead, row), :] = value

    add_rims(taps_ref, True, side_ref, part_ref, near_ref, far_ref, store)
    for i in range(8):
        block = jnp.concatenate(
            [
                estimate_ref[WIDE * x + MARGIN : WIDE * x + MARGIN + SIDE, :]
                * cols_ref[SIDE * x : SIDE * x + SIDE, :]
                for x in range(i, SIDE, 8)
            ],
            axis=0,
        )
        out_ref[pl.ds(i, Z, stride=8), :] = block.T


FLAT = (SIDE * SIDE, Z)
EDGE = (RIM * SIDE, Z)
WIDE_FLAT = (SIDE * WIDE, Z)
WIDE_EDGE = (RIM * WIDE, Z)
WIDE_RIM = (2 * RIM * SIDE, Z)
PIECES = (Z, 8, LANES)


def shards(camera_rows, blend, route, line, start, psf_xy, psf_z):
    slabs, reps = lax.axis_size("slab"), lax.axis_size("rep")
    x_tiles = LINES // SIDE
    y_tiles = slabs // x_tiles
    chunks = camera_rows.shape[0] // LANES
    pair_swaps = [(t, t ^ 1) for t in range(slabs)]
    cross_swaps = []
    for t in range(1, slabs, 2):
        if t % x_tiles != x_tiles - 1:
            cross_swaps += [(t, t + 1), (t + 1, t)]
    side = (lax.axis_index("slab") % 2).reshape(1)
    y_pairs = []
    for t in range(slabs):
        for r in range(reps):
            y = r * y_tiles + t // x_tiles + 1
            if y < y_tiles * reps:
                up = (y % y_tiles) * x_tiles + t % x_tiles
                y_pairs.append((t * reps + r, up * reps + y // y_tiles))

    def rims_x(cross, pair):
        return lax.ppermute(cross, "slab", cross_swaps), lax.ppermute(pair, "slab", pair_swaps)

    y_one, y_two = [], []
    for low, high in y_pairs:
        upward, downward = (y_one, y_two) if (low // reps) % 2 == 0 else (y_two, y_one)
        upward.append((low, high))
        downward.append((high, low))

    def rims_y(own, other):
        axes = ("slab", "rep")
        return lax.ppermute(other, axes, y_one), lax.ppermute(own, axes, y_two)

    def turn(pieces):
        return lax.all_to_all(pieces, "slab", split_axis=0, concat_axis=0, tiled=True)

    taps = psf_xy / jnp.sum(psf_xy)

    arrived = turn(call(store_tiles, [PIECES], [], start.reshape(LINES, LANES))[0])
    band = call(axial_band, [(Z, LANES)], [((8, LANES), F32)], psf_z[None, :])[0]
    rows = (
        lax.axis_index("rep").reshape(1),
        camera_rows,
        blend.reshape(chunks, LANES),
        route.reshape(chunks, LANES),
        line.reshape(chunks, LANES),
    )
    split = ((chunks * LANES, 2 * LANES), BF16)
    sent = call(
        pack_rows,
        [(CAPACITY + META, LANES)] * (OWNERS - 1),
        [split, ((CAPACITY, chunks * LANES), BF16)],
        *rows,
        smem=1,
    )
    got = [
        lax.ppermute(block, "rep", [(r, (r + step) % reps) for r in range(reps)])
        for step, block in enumerate(sent, 1)
    ]
    hot = [((LINES, CAPACITY), BF16)]
    own_hot = ((LINES, chunks * LANES), BF16)
    sums = call(begin_sums, [(LINES, LANES), (LINES, 1)], [split, own_hot], *rows, smem=1)
    for block in got[:-1]:
        sums = call(add_sums, [(LINES, LANES), (LINES, 1)], hot, block, *sums)
    seen_pieces = call(observe, [PIECES], hot + [((LINES, LANES), F32)], got[-1], *sums)[0]
    arrived, seen_pieces = lax.optimization_barrier((arrived, seen_pieces))
    estimate, flipped, *edges = call(
        arrive, [FLAT, FLAT, EDGE, EDGE], [], side, arrived.reshape(Z * 8, LANES), smem=1
    )
    seen_arrived = turn(seen_pieces)

    def own(flip, value, rows=SIDE):
        kernel = functools.partial(own_share, flip, SIDE, rows, RIM)
        return call(kernel, [(SIDE * rows, Z)], [], taps, value, smem=1)[0]

    cols = [(FLAT, F32)]
    start_rims = rims_y(*edges)
    value, *edges = call(
        along_y_first, [FLAT, EDGE, EDGE], [], taps, side, own(False, flipped), *start_rims, smem=2
    )
    blurred = call(blur, [FLAT], cols, taps, side, own(False, value), *rims_x(*edges), band, smem=2)[0]
    seen, seen_cross, seen_pair, back, *edges = call(
        first_ratio,
        [FLAT, EDGE, EDGE, FLAT, WIDE_RIM, WIDE_RIM],
        cols,
        side,
        seen_arrived.reshape(Z * 8, LANES),
        blurred,
        band,
        smem=1,
    )

    def wide_own(flip, value):
        kernel = functools.partial(own_share, flip, WIDE, SIDE, RIM + MARGIN)
        return call(kernel, [WIDE_FLAT], [], taps, value, smem=1)[0]

    near, far = rims_y(*edges)
    part = wide_own(True, back)
    seen_cross, seen_pair, part = lax.optimization_barrier((seen_cross, seen_pair, part))
    near, *seen_rims = lax.optimization_barrier((near, *rims_x(seen_cross, seen_pair)))
    near = call(near_share, [WIDE_RIM], [], taps, side, near, smem=2)[0]
    value, *edges = call(
        wide_rows, [WIDE_FLAT, WIDE_EDGE, WIDE_EDGE], [], taps, side, part, near, far, smem=2
    )
    rims = rims_x(*edges)
    wide = call(extend, [WIDE_FLAT], [], side, estimate, *start_rims, smem=1)[0]
    wide, value, *edges = call(
        update_wide,
        [WIDE_FLAT, FLAT, WIDE_RIM, WIDE_RIM],
        [(WIDE_FLAT, F32)],
        taps,
        side,
        own(True, value, WIDE),
        *rims,
        wide,
        smem=2,
    )
    rims = rims_x(*edges)
    seen = call(extend_x, [WIDE_FLAT], [], side, seen, *seen_rims, smem=1)[0]
    value, *edges = call(
        blur_ratio,
        [FLAT, EDGE, EDGE],
        [(WIDE_FLAT, F32), (WIDE_FLAT, F32)],
        taps,
        side,
        wide_own(False, value),
        *rims,
        band,
        seen,
        smem=2,
    )
    rims = rims_y(*edges)
    pieces = call(
        last_update, [(Z * 8, LANES)], cols, taps, side, own(True, value), *rims, wide, smem=2
    )[0]
    done = turn(pieces.reshape(PIECES))
    plane = call(plane_of, [(LINES, LANES)], [], done)[0]
    return plane.reshape(1, LINES, LANES)


def solution(mesh):
    in_specs = (
        P(("slab", "rep"), None),
        P(("slab", "rep")),
        P(("slab", "rep")),
        P(("slab", "rep")),
        P("slab", None, "rep"),
        P(),
        P(),
    )
    out_specs = P("slab", None, "rep")
    return jax.shard_map(shards, mesh=mesh, in_specs=in_specs, out_specs=out_specs, check_vma=False)
```
